128 devices in a mesh: grp: 8 (over z, core), sub: 16 (over x, y).
Axes of the slice: x: 4, y: 4, z: 4, core: 2. Of those that a mesh axis runs over, the one named last changes fastest.
Arguments:
- amplitudes: bfloat16 [128, 896, 896], P(('grp', 'sub')), may hold values from -0.5 to 0.5
- exchange_ints: bfloat16 [128, 896, 896], P(('grp', 'sub')), may hold values from -6 to 6
- chol: bfloat16 [8, 4096, 4096], P('grp', 'sub'), may hold values from -1.5 to 1.5
- domain: int32 [128, 7], P(('grp', 'sub')), may hold values from 0 to 31, as said below
- virt_energy: float32 [4096], replicated, may hold values from 0.5 to 4
- pair_energy: float32 [128], P(('grp', 'sub')), may hold values from -3 to -1
Outputs:
- residual: bfloat16 [128, 896, 896], P(('grp', 'sub'))
The draws below stay inside these ranges and needn't reach their ends.
Inputs may be any that keep to these rules, and one draw needn't show every extreme that they name: `domain`: each row holds 7 increasing tile numbers, no two with the same quotient by 2; rows p and p + 64 are equal.
All inputs are finite; a program needn't handle non-finite values.
Results may differ from the reference program's by a relative error of at most 0.0045.
Values may be sent and summed in bfloat16 or wider, within the bound.
No kernel may reach another device: no remote copies, remote signals or barrier semaphores. Data moves between devices by JAX's collectives and lax.ppermute only.
A program may use at most 192 MiB of HBM per device.

```python
import math
import jax
import jax.numpy as jnp
from jax import lax

TILE = 128
NVT = 32
DT = 7
V = 4096
DV = 896
PAIRS = 128
NCH = 8
N_SUB = 16


def draw_domain(key, part):
    key = jax.random.fold_in(key, 7)
    half_pairs = PAIRS // 2
    per_owner = NVT // N_SUB
    subkeys = jax.random.split(key, 2)
    pair_keys = jax.random.split(subkeys[0], half_pairs)
    shuffled = jax.vmap(lambda single: jax.random.permutation(single, N_SUB))(pair_keys)
    owners = jnp.sort(shuffled[:, :DT], axis=1)
    within = jax.random.randint(subkeys[1], (half_pairs, DT), 0, per_owner)
    first_half = (owners * per_owner + within).astype(jnp.int32)
    return jnp.concatenate([first_half, first_half], axis=0)


def steps_of(stream_key, extent, shards, low, high):
    def one(axis_at, blocks):
        steps = jax.random.uniform(jax.random.fold_in(jax.random.fold_in(stream_key, 6), axis_at), (blocks,), jnp.float32, low / len(shards), high / len(shards))
        return jnp.repeat(jnp.exp(steps), extent[axis_at] // blocks).reshape((-1,) + (1,) * (len(extent) - axis_at - 1))

    level = one(*shards[0])
    for cut in shards[1:]:
        level = level * one(*cut)
    return level


def centred(stream_key, shape, width, bound, cuts=(), kind=jnp.bfloat16):
    entries = jax.random.normal(stream_key, shape, jnp.float32) * width
    if len(cuts) > 0:
        entries = steps_of(stream_key, shape, cuts, -0.22, 0.18) * entries
    return jnp.clip(entries, min=-bound, max=bound).astype(kind)


def setup_inputs(seed: int = 0) -> dict:
    streams_of = jax.random.split(jax.random.key(seed), 7)
    return {
        "amplitudes": centred(streams_of[0], (PAIRS, DV, DV), (DV ** -0.5), 0.5, ((0, 128),)),
        "exchange_ints": centred(streams_of[1], (PAIRS, DV, DV), 1.0, 6.0, ((0, 128),)),
        "chol": centred(streams_of[2], (NCH, V, V), ((NCH * DV) ** -0.25), 1.5, ((0, 8), (1, 16))),
        "domain": draw_domain(jax.random.fold_in(streams_of[6], 71), 0),
        "virt_energy": jnp.clip(jnp.exp(jax.random.uniform(streams_of[4], (V,), jnp.float32, math.log(0.5), math.log(4.0))), 0.5, 4.0),
        "pair_energy": jnp.clip(-3.0 + 2.0 * jax.random.uniform(streams_of[5], (PAIRS,), jnp.float32) ** steps_of(streams_of[5], (PAIRS,), ((0, 128),), -0.2, 0.2), -3.0, -1.0),
    }


def domain_orbitals(pair_domain):
    offsets = jnp.arange(TILE, dtype=jnp.int32)
    return (pair_domain[:, None] * TILE + offsets[None, :]).reshape(-1).astype(jnp.int32)


def reference(amplitudes, exchange_ints, chol, domain, virt_energy, pair_energy):
    half_pairs = PAIRS // 2

    def cycle_one(pair_index):
        return jnp.dot(amplitudes[pair_index], exchange_ints[pair_index], preferred_element_type=jnp.float32).astype(jnp.bfloat16)

    cycle_terms = lax.map(cycle_one, jnp.arange(PAIRS, dtype=jnp.int32))

    def pair_one(pair_index):
        row_index = domain_orbitals(domain[pair_index])
        domain_block = jnp.take(jnp.take(chol, row_index, axis=1), row_index, axis=2)
        block_f32 = domain_block.astype(jnp.float32)
        pair_amps = amplitudes[pair_index].astype(jnp.float32)
        half_ladder = jnp.einsum('ad,qbd->qab', pair_amps, block_f32).astype(jnp.bfloat16)
        ladder = jnp.einsum('qac,qcb->ab', block_f32, half_ladder.astype(jnp.float32))
        energies = virt_energy[row_index]
        denominator = energies[:, None] + energies[None, :] - pair_energy[pair_index]
        partner = (pair_index + half_pairs) % PAIRS
        result = exchange_ints[pair_index].astype(jnp.float32) + denominator * pair_amps + ladder
        result = result + cycle_terms[pair_index].astype(jnp.float32) + cycle_terms[partner].astype(jnp.float32).T
        return result.astype(jnp.bfloat16)

    return lax.map(pair_one, jnp.arange(PAIRS, dtype=jnp.int32))
```

```python
import functools

import jax
import jax.numpy as jnp
from jax import lax
from jax.experimental import pallas as pl
from jax.experimental.pallas import tpu as pltpu
from jax.sharding import Mesh
from jax.sharding import PartitionSpec as P

TILE = 128
NVT = 32
DT = 7
DV = DT * TILE
NZ, NC, NX, NY = 4, 2, 4, 4
OWNERS = NX * NY
SLICE = TILE // OWNERS
CHIPS = NZ * OWNERS
CHUNKS = ((0, 7),)
PACK = 4


def partner_perm(to_other_core):
    pairs = []
    for z in range(NZ):
        core = 1 - z // 2
        target = 1 - core if to_other_core else core
        pairs.append((z * NC + core, (z ^ 2) * NC + target))
    return pairs


def core_swap(value):
    return lax.ppermute(value, "core", [(0, 1), (1, 0)])


def gather_small(value, axis, size):
    parts = [value]
    for step in range(1, size):
        parts.append(lax.ppermute(value, axis, [((i + step) % size, i) for i in range(size)]))
    stacked = jnp.stack(parts)
    return jnp.roll(stacked, lax.axis_index(axis), axis=0)


def pack_kernel(first, count, tiles_ref, rows_ref, out_ref):
    step = pl.program_id(0)
    for slot in range(PACK):
        dest = step * PACK + slot
        tiles = [tiles_ref[dest * DT + t] for t in range(DT)]
        columns = [pl.multiple_of(tile * TILE, TILE) for tile in tiles]
        for i in range(count):
            for j in range(DT):
                out_ref[slot, i, :, j * TILE : (j + 1) * TILE] = rows_ref[
                    tiles[first + i], :, pl.ds(columns[j], TILE)
                ]


def pack(tiles, rows, first, count):
    return pl.pallas_call(
        functools.partial(pack_kernel, first, count),
        out_shape=jax.ShapeDtypeStruct((CHIPS, count, SLICE, DV), jnp.bfloat16),
        grid_spec=pltpu.PrefetchScalarGridSpec(
            num_scalar_prefetch=1,
            grid=(CHIPS // PACK,),
            in_specs=[pl.BlockSpec((NVT, SLICE, NVT * TILE), lambda s, t: (0, 0, 0))],
            out_specs=pl.BlockSpec((PACK, count, SLICE, DV), lambda s, t: (s, 0, 0, 0)),
        ),
        compiler_params=pltpu.CompilerParams(vmem_limit_bytes=16 * 1024 * 1024),
        cost_estimate=pl.CostEstimate(
            flops=0, bytes_accessed=2 * CHIPS * count * SLICE * DV * 2, transcendentals=0
        ),
    )(tiles, rows)


def local(amplitudes, exchange_ints, chol, domain, virt_energy, pair_energy):
    z = lax.axis_index("z")
    core = lax.axis_index("core")
    home = core == z // 2
    amps, exch = amplitudes[0], exchange_ints[0]

    spread = chol.reshape(2, OWNERS, SLICE, NVT * TILE).transpose(1, 0, 2, 3)
    spread = lax.all_to_all(spread, ("x", "y"), 0, 0, tiled=True)
    rows = spread.reshape(NVT, SLICE, NVT * TILE)

    zones = lax.ppermute(domain[0], "z", [(i, i ^ 1) for i in range(NZ)])
    column = jnp.stack([jnp.where(z % 2 == 0, domain[0], zones), jnp.where(z % 2 == 0, zones, domain[0])])
    other = core_swap(column)
    column = jnp.concatenate([jnp.where(core == 0, column, other), jnp.where(core == 0, other, column)])
    everyone = gather_small(gather_small(column, "y", NY), "x", NX)
    everyone = everyone.transpose(2, 0, 1, 3).reshape(CHIPS * DT)

    moved = lax.ppermute(amps, ("z", "core"), partner_perm(True))
    mine = jnp.where(home, amps, moved)
    both = jnp.stack([mine, core_swap(mine)])

    cycle = jnp.dot(amps, exch, preferred_element_type=jnp.float32).astype(jnp.bfloat16)
    partner_cycle = lax.ppermute(cycle, ("z", "core"), partner_perm(False))

    blocks = []
    for first, count in CHUNKS:
        outgoing = pack(everyone, rows, first, count)
        arrived = lax.all_to_all(outgoing, ("z", "x", "y"), 0, 0, tiled=True)
        blocks.append(
            arrived.reshape(NZ, OWNERS, count, SLICE, DV)
            .transpose(0, 2, 1, 3, 4)
            .reshape(NZ, count * TILE, DV)
        )
    block = jnp.concatenate(blocks, axis=1) if len(blocks) > 1 else blocks[0]
    half_ladder = jnp.einsum(
        "pad,qbd->pqab", both, block, preferred_element_type=jnp.float32
    ).astype(jnp.bfloat16)
    ladder = jnp.einsum(
        "qac,pqcb->pab", block, half_ladder, preferred_element_type=jnp.float32
    )
    to_other = ladder[1] + jnp.where(home, cycle.T.astype(jnp.float32), 0.0)
    from_other = core_swap(to_other.astype(jnp.bfloat16))
    finished = ladder[0] + from_other.astype(jnp.float32)
    returned = lax.ppermute(finished.astype(jnp.bfloat16), ("z", "core"), partner_perm(True))
    added = jnp.where(
        home, finished + partner_cycle.T.astype(jnp.float32), returned.astype(jnp.float32)
    )
    energies = jnp.take(virt_energy.reshape(NVT, TILE), domain[0], axis=0).reshape(DV)
    denominator = energies[:, None] + energies[None, :] - pair_energy[0]
    result = (
        exch.astype(jnp.float32)
        + denominator * amps.astype(jnp.float32)
        + cycle.astype(jnp.float32)
        + added
    )
    return result.astype(jnp.bfloat16)[None]


def solution(mesh):
    finer = Mesh(mesh.devices.reshape(NZ, NC, NX, NY), ("z", "core", "x", "y"))
    group, everywhere = ("z", "core"), ("z", "core", "x", "y")
    placed = (
        P(everywhere, None, None),
        P(everywhere, None, None),
        P(group, ("x", "y"), None),
        P(everywhere, None),
        P(),
        P(everywhere),
    )
    return jax.shard_map(
        local, mesh=finer, in_specs=placed, out_specs=P(everywhere, None, None), check_vma=False
    )
```

```python
import functools

import jax
import jax.numpy as jnp
from jax import lax
from jax.experimental import pallas as pl
from jax.experimental.pallas import tpu as pltpu
from jax.sharding import Mesh
from jax.sharding import PartitionSpec as P

TILE = 128
NVT = 32
DT = 7
DV = DT * TILE
NZ, NC, NX, NY = 4, 2, 4, 4
OWNERS = NX * NY
SLICE = TILE // OWNERS
CHIPS = NZ * OWNERS
PACK = 4
PIECES = ((0, 2), (2, 2), (4, 3))
MIB = 1024 * 1024


def partner_perm(to_other_core):
    pairs = []
    for z in range(NZ):
        core = 1 - z // 2
        target = 1 - core if to_other_core else core
        pairs.append((z * NC + core, (z ^ 2) * NC + target))
    return pairs


def home_perm(from_home):
    pairs = [(z * NC + z // 2, z * NC + 1 - z // 2) for z in range(NZ)]
    return pairs if from_home else [(b, a) for a, b in pairs]


def core_swap(value):
    return lax.ppermute(value, "core", [(0, 1), (1, 0)])


def gather_small(value, axis, size):
    parts = [value]
    for step in range(1, size):
        parts.append(lax.ppermute(value, axis, [((i + step) % size, i) for i in range(size)]))
    stacked = jnp.stack(parts)
    return jnp.roll(stacked, lax.axis_index(axis), axis=0)


def pack_kernel(tiles_ref, rows_ref, out_ref):
    step = pl.program_id(0)
    for slot in range(PACK):
        dest = step * PACK + slot
        tiles = [tiles_ref[dest * DT + t] for t in range(DT)]
        columns = [pl.multiple_of(tile * TILE, TILE) for tile in tiles]
        for i in range(DT):
            for j in range(DT):
                out_ref[slot, i, :, j * TILE : (j + 1) * TILE] = rows_ref[
                    tiles[i], :, pl.ds(columns[j], TILE)
                ]


def pack(tiles, rows):
    return pl.pallas_call(
        pack_kernel,
        out_shape=jax.ShapeDtypeStruct((CHIPS, DT, SLICE, DV), jnp.bfloat16),
        grid_spec=pltpu.PrefetchScalarGridSpec(
            num_scalar_prefetch=1,
            grid=(CHIPS // PACK,),
            in_specs=[pl.BlockSpec((NVT, SLICE, NVT * TILE), lambda s, t: (0, 0, 0))],
            out_specs=pl.BlockSpec((PACK, DT, SLICE, DV), lambda s, t: (s, 0, 0, 0)),
        ),
        compiler_params=pltpu.CompilerParams(vmem_limit_bytes=56 * MIB),
        cost_estimate=pl.CostEstimate(
            flops=0, bytes_accessed=2 * CHIPS * DT * SLICE * DV * 2, transcendentals=0
        ),
    )(tiles, rows)


def cycle_kernel(amps_ref, exch_all_ref, exch_ref, row_ref, col_ref, base_ref, turned_ref):
    cycle = jnp.dot(amps_ref[...], exch_all_ref[...], preferred_element_type=jnp.float32)
    cycle = cycle.astype(jnp.bfloat16).astype(jnp.float32)
    denominator = col_ref[...] + row_ref[...]
    base_ref[...] = (
        exch_ref[...].astype(jnp.float32)
        + denominator * amps_ref[...].astype(jnp.float32)
        + cycle
    )
    turned_ref[...] = cycle.T.astype(jnp.bfloat16)


def cycle_and_base(amps, exch, row, col):
    return pl.pallas_call(
        cycle_kernel,
        out_shape=(
            jax.ShapeDtypeStruct((DV, DV), jnp.float32),
            jax.ShapeDtypeStruct((DV, DV), jnp.bfloat16),
        ),
        grid=(DT,),
        in_specs=[
            pl.BlockSpec((TILE, DV), lambda i: (i, 0)),
            pl.BlockSpec((DV, DV), lambda i: (0, 0)),
            pl.BlockSpec((TILE, DV), lambda i: (i, 0)),
            pl.BlockSpec((1, DV), lambda i: (0, 0)),
            pl.BlockSpec((TILE, 1), lambda i: (i, 0)),
        ],
        out_specs=(
            pl.BlockSpec((TILE, DV), lambda i: (i, 0)),
            pl.BlockSpec((DV, TILE), lambda i: (0, i)),
        ),
        compiler_params=pltpu.CompilerParams(vmem_limit_bytes=32 * MIB),
        cost_estimate=pl.CostEstimate(
            flops=2 * DV**3, bytes_accessed=14 * DV * DV, transcendentals=0
        ),
    )(amps, exch, exch, row, col)


def ladder_step(amps, block, first, count):
    half = lax.dot_general(
        amps,
        block[first * TILE : (first + count) * TILE, :],
        (((1,), (1,)), ((), ())),
        preferred_element_type=jnp.float32,
    ).astype(jnp.bfloat16)
    return jnp.dot(block, half, preferred_element_type=jnp.float32)


def first_kernel(first, count, amps_ref, arrived_ref, extra_ref, kept_ref, sent_ref, block_ref):
    step = pl.program_id(0)
    for i in range(DT):
        tile = arrived_ref[0, :, i].astype(jnp.float32).reshape(TILE, DV)
        block_ref[i * TILE : (i + 1) * TILE, :] = tile.astype(jnp.bfloat16)
    part = ladder_step(amps_ref[...], block_ref[...], first, count)

    @pl.when(step == 0)
    def _():
        kept_ref[...] = part

    @pl.when(step > 0)
    def _():
        kept_ref[...] += part

    @pl.when(step == NZ - 1)
    def _():
        sent_ref[...] = (kept_ref[...] + extra_ref[...].astype(jnp.float32)).astype(jnp.bfloat16)


def next_kernel(first, count, amps_ref, block_ref, extra_ref, kept_ref, sent_ref):
    step = pl.program_id(0)
    part = ladder_step(amps_ref[...], block_ref[...], first, count)

    @pl.when(step == 0)
    def _():
        kept_ref[...] = part

    @pl.when(step > 0)
    def _():
        kept_ref[...] += part

    @pl.when(step == NZ - 1)
    def _():
        sent_ref[...] = (kept_ref[...] + extra_ref[...].astype(jnp.float32)).astype(jnp.bfloat16)


def home_kernel(amps_ref, block_ref, base_ref, home_ref, kept_ref, sent_ref, total):
    step = pl.program_id(0)
    for first, count in PIECES:
        columns = slice(first * TILE, (first + count) * TILE)
        part = ladder_step(amps_ref[...], block_ref[...], first, count)

        @pl.when(step == 0)
        def _(part=part, columns=columns):
            total[:, columns] = part

        @pl.when(step > 0)
        def _(part=part, columns=columns):
            total[:, columns] += part

    @pl.when(step == NZ - 1)
    def _():
        sent_ref[...] = total[...].astype(jnp.bfloat16)
        keep = (home_ref[0] > 0).astype(jnp.float32)
        kept_ref[...] = base_ref[...] + keep * total[...]


def whole(shape):
    return pl.BlockSpec(shape, lambda q: (0,) * len(shape))


def cost(columns):
    return pl.CostEstimate(
        flops=4 * NZ * DV * DV * columns,
        bytes_accessed=2 * NZ * DV * DV + 8 * DV * columns,
        transcendentals=0,
    )


def first_piece(amps, arrived, extra, first, count):
    width = count * TILE
    return pl.pallas_call(
        functools.partial(first_kernel, first, count),
        out_shape=(
            jax.ShapeDtypeStruct((DV, width), jnp.float32),
            jax.ShapeDtypeStruct((DV, width), jnp.bfloat16),
            jax.ShapeDtypeStruct((DV, NZ * DV), jnp.bfloat16),
        ),
        grid=(NZ,),
        in_specs=[
            whole((DV, DV)),
            pl.BlockSpec((1, OWNERS, DT, SLICE, DV), lambda q: (q, 0, 0, 0, 0)),
            whole((DV, width)),
        ],
        out_specs=(
            whole((DV, width)),
            whole((DV, width)),
            pl.BlockSpec((DV, DV), lambda q: (0, q)),
        ),
        compiler_params=pltpu.CompilerParams(vmem_limit_bytes=40 * MIB),
        cost_estimate=cost(width),
    )(amps, arrived, extra)


def next_piece(amps, blocks, extra, first, count):
    width = count * TILE
    return pl.pallas_call(
        functools.partial(next_kernel, first, count),
        out_shape=(
            jax.ShapeDtypeStruct((DV, width), jnp.float32),
            jax.ShapeDtypeStruct((DV, width), jnp.bfloat16),
        ),
        grid=(NZ,),
        in_specs=[
            whole((DV, DV)),
            pl.BlockSpec((DV, DV), lambda q: (0, q)),
            whole((DV, width)),
        ],
        out_specs=(whole((DV, width)), whole((DV, width))),
        compiler_params=pltpu.CompilerParams(vmem_limit_bytes=40 * MIB),
        cost_estimate=cost(width),
    )(amps, blocks, extra)


def home_piece(amps, blocks, base, home):
    return pl.pallas_call(
        home_kernel,
        out_shape=(
            jax.ShapeDtypeStruct((DV, DV), jnp.float32),
            jax.ShapeDtypeStruct((DV, DV), jnp.bfloat16),
        ),
        grid=(NZ,),
        in_specs=[
            whole((DV, DV)),
            pl.BlockSpec((DV, DV), lambda q: (0, q)),
            whole((DV, DV)),
            pl.BlockSpec(memory_space=pltpu.SMEM),
        ],
        out_specs=(whole((DV, DV)), whole((DV, DV))),
        scratch_shapes=[pltpu.VMEM((DV, DV), jnp.float32)],
        compiler_params=pltpu.CompilerParams(vmem_limit_bytes=48 * MIB),
        cost_estimate=cost(DV),
    )(amps, blocks, base, home)


def local(amplitudes, exchange_ints, chol, domain, virt_energy, pair_energy):
    z = lax.axis_index("z")
    core = lax.axis_index("core")
    home = core == z // 2
    amps, exch = amplitudes[0], exchange_ints[0]
    column_group = ("z", "core")

    moved = lax.ppermute(amps, column_group, partner_perm(True))
    mine = jnp.where(home, amps, moved)
    other = core_swap(mine)
    home_amps = jnp.where(home, mine, other)
    remote_amps = jnp.where(home, other, mine)

    spread = chol.reshape(2, OWNERS, SLICE, NVT * TILE).transpose(1, 0, 2, 3)
    spread = lax.all_to_all(spread, ("x", "y"), 0, 0, tiled=True)
    rows = spread.reshape(NVT, SLICE, NVT * TILE)

    zones = lax.ppermute(domain[0], "z", [(i, i ^ 1) for i in range(NZ)])
    column = jnp.stack([jnp.where(z % 2 == 0, domain[0], zones), jnp.where(z % 2 == 0, zones, domain[0])])
    swapped = core_swap(column)
    column = jnp.concatenate([jnp.where(core == 0, column, swapped), jnp.where(core == 0, swapped, column)])
    everyone = gather_small(gather_small(column, "y", NY), "x", NX)
    everyone = everyone.transpose(2, 0, 1, 3).reshape(CHIPS * DT)

    energies = jnp.take(virt_energy.reshape(NVT, TILE), domain[0], axis=0).reshape(DV)
    base, turned = cycle_and_base(
        amps, exch, energies[None, :], (energies - pair_energy[0])[:, None]
    )
    partner_turned = lax.ppermute(turned, column_group, partner_perm(False))

    rows, home_amps, remote_amps, partner_turned = lax.optimization_barrier(
        (rows, home_amps, remote_amps, partner_turned)
    )
    base = base + partner_turned.astype(jnp.float32)

    arrived = lax.all_to_all(pack(everyone, rows), ("z", "x", "y"), 0, 0, tiled=True)
    arrived = arrived.reshape(NZ, OWNERS, DT, SLICE, DV)

    returned = []
    blocks = None
    for first, count in PIECES:
        extra = turned[:, first * TILE : (first + count) * TILE]
        if blocks is None:
            kept, sent, blocks = first_piece(remote_amps, arrived, extra, first, count)
        else:
            kept, sent = next_piece(remote_amps, blocks, extra, first, count)
        received = lax.ppermute(sent, column_group, home_perm(True))
        finished = (kept + received.astype(jnp.float32)).astype(jnp.bfloat16)
        returned.append(lax.ppermute(finished, column_group, partner_perm(True)))
    kept, sent = home_piece(home_amps, blocks, base, home.astype(jnp.int32)[None])
    received = lax.ppermute(sent, column_group, home_perm(False))
    result = (
        kept
        + received.astype(jnp.float32)
        + jnp.concatenate(returned, axis=1).astype(jnp.float32)
    )
    return result.astype(jnp.bfloat16)[None]


def solution(mesh):
    finer = Mesh(mesh.devices.reshape(NZ, NC, NX, NY), ("z", "core", "x", "y"))
    group, everywhere = ("z", "core"), ("z", "core", "x", "y")
    placed = (
        P(everywhere, None, None),
        P(everywhere, None, None),
        P(group, ("x", "y"), None),
        P(everywhere, None),
        P(),
        P(everywhere),
    )
    return jax.shard_map(
        local, mesh=finer, in_specs=placed, out_specs=P(everywhere, None, None), check_vma=False
    )
```

```python
import functools

import jax
import jax.numpy as jnp
from jax import lax
from jax.experimental import pallas as pl
from jax.experimental.pallas import tpu as pltpu
from jax.sharding import Mesh
from jax.sharding import PartitionSpec as P

TILE = 128
NVT = 32
DT = 7
DV = DT * TILE
NZ, NC, NX, NY = 4, 2, 4, 4
OWNERS = NX * NY
SLICE = TILE // OWNERS
CHIPS = NZ * OWNERS
REMOTE_PIECES = ((0, 2), (2, 2), (4, 3))
HOME_PIECES = ((0, 3), (3, 4))
MIB = 1024 * 1024


def partner_perm(to_other_core):
    pairs = []
    for z in range(NZ):
        core = 1 - z // 2
        target = 1 - core if to_other_core else core
        pairs.append((z * NC + core, (z ^ 2) * NC + target))
    return pairs


def home_perm(from_home):
    pairs = [(z * NC + z // 2, z * NC + 1 - z // 2) for z in range(NZ)]
    return pairs if from_home else [(b, a) for a, b in pairs]


def core_swap(value):
    return lax.ppermute(value, "core", [(0, 1), (1, 0)])


def gather_small(value, axis, size):
    parts = [value]
    for step in range(1, size):
        parts.append(lax.ppermute(value, axis, [((i + step) % size, i) for i in range(size)]))
    stacked = jnp.stack(parts)
    return jnp.roll(stacked, lax.axis_index(axis), axis=0)


def pack_kernel(tiles_ref, given_ref, out_ref, rows_ref, packed, row_sems, sems):
    fetches = []
    for k in range(NVT // 4):
        part = pl.ds(k * 4, 4)
        fetches.append(pltpu.make_async_copy(given_ref.at[part], rows_ref.at[part], row_sems.at[k]))
    for fetch in fetches:
        fetch.start()
    for fetch in fetches:
        fetch.wait()

    def one(dest, carry):
        tiles = [tiles_ref[dest * DT + t] for t in range(DT)]
        columns = [pl.multiple_of(tile * TILE, TILE) for tile in tiles]
        for i in range(DT):
            for j in range(DT):
                packed[dest, i, :, j * TILE : (j + 1) * TILE] = rows_ref[
                    tiles[i], :, pl.ds(columns[j], TILE)
                ]
        pltpu.make_async_copy(packed.at[dest], out_ref.at[dest], sems.at[dest]).start()
        return carry

    def finish(dest, carry):
        pltpu.make_async_copy(packed.at[dest], out_ref.at[dest], sems.at[dest]).wait()
        return carry

    lax.fori_loop(0, CHIPS, one, 0)
    lax.fori_loop(0, CHIPS, finish, 0)


def pack(tiles, rows):
    shape = (CHIPS, DT, SLICE, DV)
    return pl.pallas_call(
        pack_kernel,
        out_shape=jax.ShapeDtypeStruct(shape, jnp.bfloat16),
        in_specs=[
            pl.BlockSpec(memory_space=pltpu.SMEM),
            pl.BlockSpec(memory_space=pl.ANY),
        ],
        out_specs=pl.BlockSpec(memory_space=pl.ANY),
        scratch_shapes=[
            pltpu.VMEM(rows.shape, jnp.bfloat16),
            pltpu.VMEM(shape, jnp.bfloat16),
            pltpu.SemaphoreType.DMA((NVT // 4,)),
            pltpu.SemaphoreType.DMA((CHIPS,)),
        ],
        compiler_params=pltpu.CompilerParams(vmem_limit_bytes=56 * MIB),
        cost_estimate=pl.CostEstimate(
            flops=0, bytes_accessed=2 * CHIPS * DT * SLICE * DV * 2, transcendentals=0
        ),
    )(tiles, rows)


def cycle_kernel(
    amps_ref, exch_all_ref, exch_ref, row_ref, col_ref, after_ref, base_ref, turned_ref
):
    del after_ref
    cycle = jnp.dot(amps_ref[...], exch_all_ref[...], preferred_element_type=jnp.float32)
    cycle = cycle.astype(jnp.bfloat16).astype(jnp.float32)
    denominator = col_ref[...] + row_ref[...]
    base_ref[...] = (
        exch_ref[...].astype(jnp.float32)
        + denominator * amps_ref[...].astype(jnp.float32)
        + cycle
    )
    turned_ref[...] = cycle.T.astype(jnp.bfloat16)


def cycle_and_base(amps, exch, row, col, after):
    return pl.pallas_call(
        cycle_kernel,
        out_shape=(
            jax.ShapeDtypeStruct((DV, DV), jnp.float32),
            jax.ShapeDtypeStruct((DV, DV), jnp.bfloat16),
        ),
        grid=(DT,),
        in_specs=[
            pl.BlockSpec((TILE, DV), lambda i: (i, 0)),
            pl.BlockSpec((DV, DV), lambda i: (0, 0)),
            pl.BlockSpec((TILE, DV), lambda i: (i, 0)),
            pl.BlockSpec((1, DV), lambda i: (0, 0)),
            pl.BlockSpec((TILE, 1), lambda i: (i, 0)),
            pl.BlockSpec(memory_space=pl.ANY),
        ],
        out_specs=(
            pl.BlockSpec((TILE, DV), lambda i: (i, 0)),
            pl.BlockSpec((DV, TILE), lambda i: (0, i)),
        ),
        compiler_params=pltpu.CompilerParams(vmem_limit_bytes=32 * MIB),
        cost_estimate=pl.CostEstimate(
            flops=2 * DV**3, bytes_accessed=14 * DV * DV, transcendentals=0
        ),
    )(amps, exch, exch, row, col, after)


def whole(shape):
    return pl.BlockSpec(shape, lambda q: (0,) * len(shape))


def ladder_kernel(first, count, raw, home, *refs):
    refs = list(refs)
    amps = [refs.pop(0) for _ in range(DT)]
    given = [refs.pop(0) for _ in range(DT)]
    if home:
        base_ref, home_ref = refs.pop(0), refs.pop(0)
    else:
        extra_ref = refs.pop(0)
    refs.pop(0)
    kept_ref, sent_ref = refs.pop(0), refs.pop(0)
    block_ref = refs.pop(0) if raw else None
    half, total = refs.pop(0), refs.pop(0)
    step = pl.program_id(0)
    if home:
        base, base_sem = refs.pop(0), refs.pop(0)
        columns = pl.ds(first * TILE, count * TILE)
        fetch = pltpu.make_async_copy(base_ref.at[:, columns], base, base_sem)

        @pl.when(step == 0)
        def _():
            fetch.start()

    if raw:
        for i in range(DT):
            tile = given[i][0, :, 0].astype(jnp.float32).reshape(TILE, DV)
            block_ref[i * TILE : (i + 1) * TILE, :] = tile.astype(jnp.bfloat16)
        rows = [block_ref.at[i * TILE : (i + 1) * TILE, :] for i in range(DT)]
    else:
        rows = given
    for start in range(first, first + count, 2):
        some = range(start, min(start + 2, first + count))
        right = jnp.concatenate([rows[t][...] for t in some], axis=0)
        place = slice((start - first) * TILE, (some[-1] + 1 - first) * TILE)
        for c in range(DT):
            half[c * TILE : (c + 1) * TILE, place] = lax.dot_general(
                amps[c][...], right, (((1,), (1,)), ((), ())), preferred_element_type=jnp.float32
            ).astype(jnp.bfloat16)

    @pl.when(step == 0)
    def _():
        for i in range(DT):
            total[i * TILE : (i + 1) * TILE, :] = jnp.dot(
                rows[i][...], half[...], preferred_element_type=jnp.float32
            )

    @pl.when(step > 0)
    def _():
        for i in range(DT):
            total[i * TILE : (i + 1) * TILE, :] += jnp.dot(
                rows[i][...], half[...], preferred_element_type=jnp.float32
            )

    @pl.when(step == NZ - 1)
    def _():
        if home:
            fetch.wait()
            keep = (home_ref[0] > 0).astype(jnp.float32)
            sent_ref[...] = total[...].astype(jnp.bfloat16)
            kept_ref[...] = base[...] + keep * total[...]
        else:
            kept_ref[...] = total[...]
            sent_ref[...] = (total[...] + extra_ref[...].astype(jnp.float32)).astype(jnp.bfloat16)


def ladder_piece(amps, blocks, added, first, count, after, home=None):
    raw = blocks.ndim == 5
    width = count * TILE
    if raw:
        given = [
            pl.BlockSpec((1, OWNERS, 1, SLICE, DV), lambda q, i=i: (q, 0, i, 0, 0)) for i in range(DT)
        ]
    else:
        given = [pl.BlockSpec((TILE, DV), lambda q, i=i: (i, q)) for i in range(DT)]
    anywhere = pl.BlockSpec(memory_space=pl.ANY)
    scratch = [pltpu.VMEM((DV, width), jnp.bfloat16), pltpu.VMEM((DV, width), jnp.float32)]
    out_shape = [
        jax.ShapeDtypeStruct((DV, width), jnp.float32),
        jax.ShapeDtypeStruct((DV, width), jnp.bfloat16),
    ]
    out_specs = [whole((DV, width)), whole((DV, width))]
    if raw:
        out_shape.append(jax.ShapeDtypeStruct((DV, NZ * DV), jnp.bfloat16))
        out_specs.append(pl.BlockSpec((DV, DV), lambda q: (0, q)))
    if home is None:
        more, more_specs = [added], [whole((DV, width))]
    else:
        more, more_specs = [added, home], [anywhere, pl.BlockSpec(memory_space=pltpu.SMEM)]
        scratch += [pltpu.VMEM((DV, width), jnp.float32), pltpu.SemaphoreType.DMA]
    return pl.pallas_call(
        functools.partial(ladder_kernel, first, count, raw, home is not None),
        out_shape=out_shape,
        grid=(NZ,),
        in_specs=[pl.BlockSpec((TILE, DV), lambda q, i=i: (i, 0)) for i in range(DT)]
        + given
        + more_specs
        + [anywhere],
        out_specs=out_specs,
        scratch_shapes=scratch,
        compiler_params=pltpu.CompilerParams(vmem_limit_bytes=36 * MIB),
        cost_estimate=pl.CostEstimate(
            flops=4 * NZ * DV * DV * width,
            bytes_accessed=2 * NZ * DV * DV + 8 * DV * width,
            transcendentals=0,
        ),
    )(*[amps] * DT, *[blocks] * DT, *more, after)


def local(amplitudes, exchange_ints, chol, domain, virt_energy, pair_energy):
    z = lax.axis_index("z")
    core = lax.axis_index("core")
    home = core == z // 2
    amps, exch = amplitudes[0], exchange_ints[0]
    column_group = ("z", "core")

    moved = lax.ppermute(amps, column_group, partner_perm(True))
    mine = jnp.where(home, amps, moved)
    other = core_swap(mine)
    home_amps = jnp.where(home, mine, other)
    remote_amps = jnp.where(home, other, mine)

    spread = chol.reshape(2, OWNERS, SLICE, NVT * TILE).transpose(1, 0, 2, 3)
    spread = lax.all_to_all(spread, ("x", "y"), 0, 0, tiled=True)
    rows = spread.reshape(NVT, SLICE, NVT * TILE)

    zones = lax.ppermute(domain[0], "z", [(i, i ^ 1) for i in range(NZ)])
    column = jnp.stack([jnp.where(z % 2 == 0, domain[0], zones), jnp.where(z % 2 == 0, zones, domain[0])])
    swapped = core_swap(column)
    column = jnp.concatenate([jnp.where(core == 0, column, swapped), jnp.where(core == 0, swapped, column)])
    row_of_chips = gather_small(column, "y", NY)
    everyone = gather_small(row_of_chips, "x", NX)
    everyone = everyone.transpose(2, 0, 1, 3).reshape(CHIPS * DT)

    energies = jnp.take(virt_energy.reshape(NVT, TILE), domain[0], axis=0).reshape(DV)
    base, turned = cycle_and_base(
        amps, exch, energies[None, :], (energies - pair_energy[0])[:, None], row_of_chips
    )
    partner_turned = lax.ppermute(turned, column_group, partner_perm(False))
    base = base + partner_turned.astype(jnp.float32)

    arrived = lax.all_to_all(pack(everyone, rows), ("z", "x", "y"), 0, 0, tiled=True)
    blocks = arrived.reshape(NZ, OWNERS, DT, SLICE, DV)

    finished = []
    for k, (first, count) in enumerate(REMOTE_PIECES):
        extra = turned[:, first * TILE : (first + count) * TILE]
        after = finished[k - 2] if k >= 2 else domain
        parts = ladder_piece(remote_amps, blocks, extra, first, count, after)
        if k == 0:
            blocks = parts[2]
        received = lax.ppermute(parts[1], column_group, home_perm(True))
        finished.append((parts[0] + received.astype(jnp.float32)).astype(jnp.bfloat16))
    returned = [lax.ppermute(piece, column_group, partner_perm(True)) for piece in finished]

    results = []
    for k, (first, count) in enumerate(HOME_PIECES):
        after = finished[len(REMOTE_PIECES) - 2 + k]
        kept, sent = ladder_piece(
            home_amps, blocks, base, first, count, after, home.astype(jnp.int32)[None]
        )
        received = lax.ppermute(sent, column_group, home_perm(False))
        results.append(kept + received.astype(jnp.float32))
    result = jnp.concatenate(results, axis=1) + jnp.concatenate(returned, axis=1).astype(jnp.float32)
    return result.astype(jnp.bfloat16)[None]


def solution(mesh):
    finer = Mesh(mesh.devices.reshape(NZ, NC, NX, NY), ("z", "core", "x", "y"))
    group, everywhere = ("z", "core"), ("z", "core", "x", "y")
    placed = (
        P(everywhere, None, None),
        P(everywhere, None, None),
        P(group, ("x", "y"), None),
        P(everywhere, None),
        P(),
        P(everywhere),
    )
    return jax.shard_map(
        local, mesh=finer, in_specs=placed, out_specs=P(everywhere, None, None), check_vma=False
    )
```

```python
import functools

import jax
import jax.numpy as jnp
from jax import lax
from jax.experimental import pallas as pl
from jax.experimental.pallas import tpu as pltpu
from jax.sharding import Mesh
from jax.sharding import PartitionSpec as P

TILE = 128
NVT = 32
DT = 7
DV = DT * TILE
NZ, NC, NX, NY = 4, 2, 4, 4
OWNERS = NX * NY
SLICE = TILE // OWNERS
CHIPS = NZ * OWNERS
PIECES = ((0, 4), (4, 3))
MIB = 1024 * 1024


def partner_perm(to_other_core):
    pairs = []
    for z in range(NZ):
        core = 1 - z // 2
        target = 1 - core if to_other_core else core
        pairs.append((z * NC + core, (z ^ 2) * NC + target))
    return pairs


def home_perm(from_home):
    pairs = [(z * NC + z // 2, z * NC + 1 - z // 2) for z in range(NZ)]
    return pairs if from_home else [(b, a) for a, b in pairs]


def core_swap(value):
    return lax.ppermute(value, "core", [(0, 1), (1, 0)])


def spread_kernel(chol_ref, table_ref, out_ref, staged, in_sems, out_sems):
    arriving, leaving = [], []
    for m in range(OWNERS):
        for t in range(2):
            arriving.append(
                pltpu.make_async_copy(
                    chol_ref.at[t * OWNERS + m], staged.at[m, t, :, 0 : NVT * TILE], in_sems.at[m, t]
                )
            )
            leaving.append(
                pltpu.make_async_copy(staged.at[m, t], out_ref.at[m, t], out_sems.at[m, t])
            )
    for copy in arriving:
        copy.start()
    for m in range(OWNERS):
        for t in range(2):
            staged[m, t, :, NVT * TILE :] = table_ref[...]
            arriving[2 * m + t].wait()
            leaving[2 * m + t].start()
    for copy in leaving:
        copy.wait()


def spread(chol, table):
    return pl.pallas_call(
        spread_kernel,
        out_shape=jax.ShapeDtypeStruct((OWNERS, 2, SLICE, (NVT + 1) * TILE), jnp.bfloat16),
        in_specs=[pl.BlockSpec(memory_space=pl.ANY), pl.BlockSpec(memory_space=pltpu.VMEM)],
        out_specs=pl.BlockSpec(memory_space=pl.ANY),
        scratch_shapes=[
            pltpu.VMEM((OWNERS, 2, SLICE, (NVT + 1) * TILE), jnp.bfloat16),
            pltpu.SemaphoreType.DMA((OWNERS, 2)),
            pltpu.SemaphoreType.DMA((OWNERS, 2)),
        ],
        compiler_params=pltpu.CompilerParams(vmem_limit_bytes=56 * MIB),
    )(chol, table)


def pack_kernel(given_ref, out_ref, rows_ref, tables, tiles_ref, packed, row_sems, table_sem, sems):
    fetches = []
    for k in range(NVT // 4):
        part = pl.ds(k * 4, 4)
        fetches.append(pltpu.make_async_copy(given_ref.at[part], rows_ref.at[part], row_sems.at[k]))
    for fetch in fetches:
        fetch.start()
    for fetch in fetches:
        fetch.wait()
    for s in range(OWNERS):
        table = rows_ref[2 * s, :, NVT * TILE :].astype(jnp.float32).astype(jnp.int32)
        tables[s : s + 1, :] = table[0:1, :]
    move = pltpu.make_async_copy(tables, tiles_ref, table_sem)
    move.start()
    move.wait()

    def one(s, carry):
        for z in range(NZ):
            dest = z * OWNERS + s
            tiles = [tiles_ref[s, z * DT + t] for t in range(DT)]
            columns = [pl.multiple_of(tile * TILE, TILE) for tile in tiles]
            for i in range(DT):
                for j in range(DT):
                    packed[dest, i, :, j * TILE : (j + 1) * TILE] = rows_ref[
                        tiles[i], :, pl.ds(columns[j], TILE)
                    ]
            pltpu.make_async_copy(packed.at[dest], out_ref.at[dest], sems.at[dest]).start()
        return carry

    def finish(dest, carry):
        pltpu.make_async_copy(packed.at[dest], out_ref.at[dest], sems.at[dest]).wait()
        return carry

    lax.fori_loop(0, OWNERS, one, 0)
    lax.fori_loop(0, CHIPS, finish, 0)


def pack(rows):
    shape = (CHIPS, DT, SLICE, DV)
    return pl.pallas_call(
        pack_kernel,
        out_shape=jax.ShapeDtypeStruct(shape, jnp.bfloat16),
        in_specs=[pl.BlockSpec(memory_space=pl.ANY)],
        out_specs=pl.BlockSpec(memory_space=pl.ANY),
        scratch_shapes=[
            pltpu.VMEM(rows.shape, jnp.bfloat16),
            pltpu.VMEM((OWNERS, TILE), jnp.int32),
            pltpu.SMEM((OWNERS, TILE), jnp.int32),
            pltpu.VMEM(shape, jnp.bfloat16),
            pltpu.SemaphoreType.DMA((NVT // 4,)),
            pltpu.SemaphoreType.DMA,
            pltpu.SemaphoreType.DMA((CHIPS,)),
        ],
        compiler_params=pltpu.CompilerParams(vmem_limit_bytes=56 * MIB),
        cost_estimate=pl.CostEstimate(
            flops=0, bytes_accessed=2 * CHIPS * DT * SLICE * DV * 2, transcendentals=0
        ),
    )(rows)


def cycle_kernel(amps_ref, exch_all_ref, exch_ref, row_ref, col_ref, *refs):
    cycle = jnp.dot(amps_ref[...], exch_all_ref[...], preferred_element_type=jnp.float32)
    cycle = cycle.astype(jnp.bfloat16).astype(jnp.float32)
    denominator = col_ref[...] + row_ref[...]
    base = (
        exch_ref[...].astype(jnp.float32)
        + denominator * amps_ref[...].astype(jnp.float32)
        + cycle
    )
    turned = cycle.T.astype(jnp.bfloat16)
    step = pl.program_id(0)
    for k, (first, count) in enumerate(PIECES):
        refs[1 + k][...] = base[:, first * TILE : (first + count) * TILE]

        @pl.when(jnp.logical_and(step >= first, step < first + count))
        def _(k=k):
            refs[1 + len(PIECES) + k][...] = turned


def cycle_and_base(amps, exch, row, col, after):
    def turned_place(first, count):
        return lambda i: (0, jnp.clip(i - first, 0, count - 1))

    widths = [count * TILE for _, count in PIECES]
    return pl.pallas_call(
        cycle_kernel,
        out_shape=[jax.ShapeDtypeStruct((DV, width), jnp.float32) for width in widths]
        + [jax.ShapeDtypeStruct((DV, width), jnp.bfloat16) for width in widths],
        grid=(DT,),
        in_specs=[
            pl.BlockSpec((TILE, DV), lambda i: (i, 0)),
            pl.BlockSpec((DV, DV), lambda i: (0, 0)),
            pl.BlockSpec((TILE, DV), lambda i: (i, 0)),
            pl.BlockSpec((1, DV), lambda i: (0, 0)),
            pl.BlockSpec((TILE, 1), lambda i: (i, 0)),
            pl.BlockSpec(memory_space=pl.ANY),
        ],
        out_specs=[pl.BlockSpec((TILE, width), lambda i: (i, 0)) for width in widths]
        + [pl.BlockSpec((DV, TILE), turned_place(*piece)) for piece in PIECES],
        compiler_params=pltpu.CompilerParams(vmem_limit_bytes=32 * MIB),
        cost_estimate=pl.CostEstimate(
            flops=2 * DV**3, bytes_accessed=14 * DV * DV, transcendentals=0
        ),
    )(amps, exch, exch, row, col, after)


def choose_kernel(home_ref, *refs):
    sources, targets, sems = refs[:4], refs[4:6], refs[6]
    home = home_ref[0] > 0

    def copies(which):
        made = []
        for k in range(2):
            for i in range(DT):
                part = pl.ds(i * TILE, TILE)
                made.append(
                    pltpu.make_async_copy(
                        sources[2 * which + k].at[part], targets[k].at[part], sems.at[k, i]
                    )
                )
        return made

    for which in range(2):

        @pl.when(home if which == 0 else jnp.logical_not(home))
        def _(which=which):
            made = copies(which)
            for copy in made:
                copy.start()
            for copy in made:
                copy.wait()


def choose(home, at_home, elsewhere):
    vmem = pl.BlockSpec(memory_space=pltpu.VMEM)
    return pl.pallas_call(
        choose_kernel,
        out_shape=[pltpu.VMEM((DV, DV), jnp.bfloat16)] * 2,
        in_specs=[pl.BlockSpec(memory_space=pltpu.SMEM)] + [pl.BlockSpec(memory_space=pl.ANY)] * 4,
        out_specs=[vmem, vmem],
        scratch_shapes=[pltpu.SemaphoreType.DMA((2, DT))],
        compiler_params=pltpu.CompilerParams(vmem_limit_bytes=8 * MIB),
    )(home, *at_home, *elsewhere)


def ladder_kernel(first, count, raw, home, amps_ref, given_ref, added_ref, *refs):
    refs = list(refs)
    base_ref = refs.pop(0) if home else None
    home_ref = refs.pop(0) if home else None
    refs.pop(0)
    kept_ref, sent_ref = refs.pop(0), refs.pop(0)
    block_ref = refs.pop(0) if raw else given_ref
    half, total = refs.pop(0), refs.pop(0)
    if raw:
        landed, sems = refs.pop(0), refs.pop(0)
        copies = [
            [
                pltpu.make_async_copy(given_ref.at[q, :, i], landed.at[q, i], sems.at[q, i])
                for i in range(DT)
            ]
            for q in range(NZ)
        ]
        for q in range(NZ):
            for copy in copies[q]:
                copy.start()
    for q in range(NZ):
        if raw:
            for i in range(DT):
                copies[q][i].wait()
                tile = landed[q, i].astype(jnp.float32).reshape(TILE, DV)
                block_ref[q, i * TILE : (i + 1) * TILE, :] = tile.astype(jnp.bfloat16)
        for start in range(first, first + count, 2):
            stop = min(start + 2, first + count)
            half[:, (start - first) * TILE : (stop - first) * TILE] = lax.dot_general(
                amps_ref[...],
                block_ref[q, start * TILE : stop * TILE, :],
                (((1,), (1,)), ((), ())),
                preferred_element_type=jnp.float32,
            ).astype(jnp.bfloat16)
        for i in range(DT):
            place = slice(i * TILE, (i + 1) * TILE)
            part = jnp.dot(
                block_ref[q, place, :], half[...], preferred_element_type=jnp.float32
            )
            if q > 0:
                part = part + total[place, :]
            if q < NZ - 1:
                total[place, :] = part
            elif home:
                keep = (home_ref[0] > 0).astype(jnp.float32)
                sent_ref[place, :] = part.astype(jnp.bfloat16)
                added = base_ref[place, :] + added_ref[place, :].astype(jnp.float32)
                kept_ref[place, :] = added + keep * part
            else:
                kept_ref[place, :] = part
                sent_ref[place, :] = (part + added_ref[place, :].astype(jnp.float32)).astype(
                    jnp.bfloat16
                )


def in_vmem(value):
    return pltpu.with_memory_space_constraint(value, pltpu.VMEM)


def ladder_piece(amps, blocks, added, first, count, after, base=None, home=None):
    raw = blocks.ndim == 5
    width = count * TILE
    vmem = pl.BlockSpec(memory_space=pltpu.VMEM)
    anywhere = pl.BlockSpec(memory_space=pl.ANY)
    scratch = [pltpu.VMEM((DV, width), jnp.bfloat16), pltpu.VMEM((DV, width), jnp.float32)]
    out_shape = [
        pltpu.VMEM((DV, width), jnp.float32),
        pltpu.VMEM((DV, width), jnp.bfloat16),
    ]
    if raw:
        out_shape.append(pltpu.VMEM((NZ, DV, DV), jnp.bfloat16))
        scratch += [
            pltpu.VMEM((NZ, DT, OWNERS, SLICE, DV), jnp.bfloat16),
            pltpu.SemaphoreType.DMA((NZ, DT)),
        ]
    operands = [in_vmem(amps), blocks if raw else in_vmem(blocks), in_vmem(added)]
    specs = [vmem, anywhere if raw else vmem, vmem]
    if home is not None:
        operands += [in_vmem(base), home]
        specs += [vmem, pl.BlockSpec(memory_space=pltpu.SMEM)]
    return pl.pallas_call(
        functools.partial(ladder_kernel, first, count, raw, home is not None),
        out_shape=out_shape,
        in_specs=specs + [anywhere],
        out_specs=[vmem] * len(out_shape),
        scratch_shapes=scratch,
        compiler_params=pltpu.CompilerParams(vmem_limit_bytes=16 * MIB),
        cost_estimate=pl.CostEstimate(
            flops=4 * NZ * DV * DV * width,
            bytes_accessed=2 * NZ * DV * DV + 8 * DV * width,
            transcendentals=0,
        ),
    )(*operands, after)


def local(amplitudes, exchange_ints, chol, domain, virt_energy, pair_energy):
    z = lax.axis_index("z")
    core = lax.axis_index("core")
    home = core == z // 2
    amps, exch = amplitudes[0], exchange_ints[0]
    column_group = ("z", "core")

    zones = lax.ppermute(domain[0], "z", [(i, i ^ 1) for i in range(NZ)])
    column = jnp.stack([jnp.where(z % 2 == 0, domain[0], zones), jnp.where(z % 2 == 0, zones, domain[0])])
    swapped = core_swap(column)
    column = jnp.concatenate([jnp.where(core == 0, column, swapped), jnp.where(core == 0, swapped, column)])
    table = column.reshape(1, NZ * DT).astype(jnp.bfloat16)
    table = jnp.pad(table, ((0, SLICE - 1), (0, TILE - NZ * DT)))

    outgoing = spread(chol.reshape(2 * OWNERS, SLICE, NVT * TILE), table)
    rows = lax.all_to_all(outgoing, ("x", "y"), 0, 0, tiled=True)
    rows = rows.reshape(NVT, SLICE, (NVT + 1) * TILE)

    energies = jnp.take(virt_energy.reshape(NVT, TILE), domain[0], axis=0).reshape(DV)
    parts = cycle_and_base(
        amps, exch, energies[None, :], (energies - pair_energy[0])[:, None], outgoing
    )
    bases, turned = parts[: len(PIECES)], parts[len(PIECES) :]
    partner_turned = [lax.ppermute(piece, column_group, partner_perm(False)) for piece in turned]

    early, _ = lax.optimization_barrier((amps, outgoing))
    moved = lax.ppermute(early, column_group, partner_perm(True))
    home_amps, _ = lax.optimization_barrier((amps, turned[0]))
    home_amps = lax.ppermute(home_amps, column_group, home_perm(True))
    moved, _ = lax.optimization_barrier((moved, turned[0]))
    remote_amps = lax.ppermute(moved, column_group, home_perm(False))
    is_home = home.astype(jnp.int32)[None]
    home_amps, remote_amps = choose(is_home, (amps, remote_amps), (home_amps, moved))

    rows, home_amps, remote_amps, *partner_turned = lax.optimization_barrier(
        (rows, home_amps, remote_amps, *partner_turned)
    )

    arrived = lax.all_to_all(pack(rows), ("z", "x", "y"), 0, 0, tiled=True)
    blocks = arrived.reshape(NZ, OWNERS, DT, SLICE, DV)

    returned, waiting = [], None
    for k, (first, count) in enumerate(PIECES):
        kept, sent, *natural = ladder_piece(remote_amps, blocks, turned[k], first, count, domain)
        if natural:
            blocks = natural[0]
        received = lax.ppermute(sent, column_group, home_perm(True))
        if k < len(PIECES) - 1:
            finished = (kept + received.astype(jnp.float32)).astype(jnp.bfloat16)
            returned.append(lax.ppermute(finished, column_group, partner_perm(True)))

    results = []
    after = [sent, returned[0]]
    for k, (first, count) in enumerate(PIECES):
        held, sent = ladder_piece(
            home_amps, blocks, partner_turned[k], first, count, after[k], bases[k], is_home
        )
        if k == 0:
            kept, _ = lax.optimization_barrier((kept, sent))
            finished = (kept + received.astype(jnp.float32)).astype(jnp.bfloat16)
            returned.append(lax.ppermute(finished, column_group, partner_perm(True)))
        else:
            sent, *returned = lax.optimization_barrier((sent, *returned))
        results.append((held, lax.ppermute(sent, column_group, home_perm(False))))
    result = [
        held + came.astype(jnp.float32) + back.astype(jnp.float32)
        for (held, came), back in zip(results, returned)
    ]
    return jnp.concatenate(result, axis=1).astype(jnp.bfloat16)[None]


def solution(mesh):
    finer = Mesh(mesh.devices.reshape(NZ, NC, NX, NY), ("z", "core", "x", "y"))
    group, everywhere = ("z", "core"), ("z", "core", "x", "y")
    placed = (
        P(everywhere, None, None),
        P(everywhere, None, None),
        P(group, ("x", "y"), None),
        P(everywhere, None),
        P(),
        P(everywhere),
    )
    return jax.shard_map(
        local, mesh=finer, in_specs=placed, out_specs=P(everywhere, None, None), check_vma=False
    )
```

```python
import functools

import jax
import jax.numpy as jnp
from jax import lax
from jax.experimental import pallas as pl
from jax.experimental.pallas import tpu as pltpu
from jax.sharding import Mesh
from jax.sharding import PartitionSpec as P

TILE = 128
NVT = 32
DT = 7
DV = DT * TILE
NZ, NC, NX, NY = 4, 2, 4, 4
OWNERS = NX * NY
SLICE = TILE // OWNERS
CHIPS = NZ * OWNERS
AFTER = 3
CUT = 4
GROUP = 4
MIB = 1024 * 1024


def partner_perm(to_other_core):
    pairs = []
    for z in range(NZ):
        core = 1 - z // 2
        target = 1 - core if to_other_core else core
        pairs.append((z * NC + core, (z ^ 2) * NC + target))
    return pairs


def home_perm(from_home):
    pairs = [(z * NC + z // 2, z * NC + 1 - z // 2) for z in range(NZ)]
    return pairs if from_home else [(b, a) for a, b in pairs]


def core_swap(value):
    return lax.ppermute(value, "core", [(0, 1), (1, 0)])


def in_hbm(value):
    return pltpu.with_memory_space_constraint(value, pltpu.HBM)


def spread_kernel(chol_ref, out_ref, staged, in_sems, out_sems):
    arriving, leaving = [], []
    for m in range(OWNERS):
        for t in range(2):
            place = (m, t, slice(None), slice(0, NVT * TILE))
            arriving.append(
                pltpu.make_async_copy(
                    chol_ref.at[t * OWNERS + m], staged.at[m, t], in_sems.at[m, t]
                )
            )
            leaving.append(
                pltpu.make_async_copy(staged.at[m, t], out_ref.at[place], out_sems.at[m, t])
            )
    for copy in arriving:
        copy.start()
    for come, leave in zip(arriving, leaving):
        come.wait()
        leave.start()
    for copy in leaving:
        copy.wait()


def spread(chol):
    return pl.pallas_call(
        spread_kernel,
        out_shape=pltpu.HBM((OWNERS, 2, SLICE, (NVT + 1) * TILE), jnp.bfloat16),
        in_specs=[pl.BlockSpec(memory_space=pl.ANY)],
        out_specs=pl.BlockSpec(memory_space=pl.ANY),
        scratch_shapes=[
            pltpu.VMEM((OWNERS, 2, SLICE, NVT * TILE), jnp.bfloat16),
            pltpu.SemaphoreType.DMA((OWNERS, 2)),
            pltpu.SemaphoreType.DMA((OWNERS, 2)),
        ],
        compiler_params=pltpu.CompilerParams(vmem_limit_bytes=30 * MIB),
        cost_estimate=pl.CostEstimate(flops=0, bytes_accessed=4 * MIB, transcendentals=0),
    )(in_hbm(chol))


def table_kernel(table_ref, given_ref, out_ref, sems):
    del given_ref
    copies = []
    for m in range(OWNERS):
        for t in range(2):
            copies.append(
                pltpu.make_async_copy(
                    table_ref, out_ref.at[m, t, :, pl.ds(NVT * TILE, TILE)], sems.at[m, t]
                )
            )
    for copy in copies:
        copy.start()
    for copy in copies:
        copy.wait()


def with_table(spread_rows, table):
    anywhere = pl.BlockSpec(memory_space=pl.ANY)
    return pl.pallas_call(
        table_kernel,
        out_shape=pltpu.HBM(spread_rows.shape, jnp.bfloat16),
        in_specs=[pl.BlockSpec(memory_space=pltpu.VMEM), anywhere],
        out_specs=anywhere,
        scratch_shapes=[pltpu.SemaphoreType.DMA((OWNERS, 2))],
        input_output_aliases={1: 0},
        compiler_params=pltpu.CompilerParams(vmem_limit_bytes=8 * MIB),
    )(table, in_hbm(spread_rows))


def pack_kernel(given_ref, *refs):
    out_ref, rows_ref, given_tables, tables, tiles_ref, packed, row_sems, table_sems, sems = refs[AFTER:]
    beside = pltpu.make_async_copy(
        given_ref.at[:, :, pl.ds(NVT * TILE, TILE)], given_tables, table_sems.at[0]
    )
    beside.start()
    fetches = []
    for k in range(NVT // 4):
        part = pl.ds(k * 4, 4)
        fetches.append(
            pltpu.make_async_copy(
                given_ref.at[part, :, pl.ds(0, NVT * TILE)], rows_ref.at[part], row_sems.at[k]
            )
        )
    for fetch in fetches:
        fetch.start()
    beside.wait()
    for s in range(OWNERS):
        table = given_tables[2 * s].astype(jnp.float32).astype(jnp.int32)
        tables[s : s + 1, :] = table[0:1, :]
    move = pltpu.make_async_copy(tables, tiles_ref, table_sems.at[1])
    move.start()
    move.wait()
    for fetch in fetches:
        fetch.wait()

    def leave(group):
        dests = pl.ds(group * GROUP, GROUP)
        return pltpu.make_async_copy(packed.at[dests], out_ref.at[dests], sems.at[group])

    def one(group, carry):
        for k in range(GROUP):
            dest = group * GROUP + k
            z, s = dest // OWNERS, dest % OWNERS
            tiles = [tiles_ref[s, z * DT + t] for t in range(DT)]
            columns = [pl.multiple_of(tile * TILE, TILE) for tile in tiles]
            for i in range(DT):
                for j in range(DT):
                    packed[dest, i, :, j * TILE : (j + 1) * TILE] = rows_ref[
                        tiles[i], :, pl.ds(columns[j], TILE)
                    ]
        leave(group).start()
        return carry

    def gone(group, carry):
        leave(group).wait()
        return carry

    lax.fori_loop(0, CHIPS // GROUP, one, 0)
    lax.fori_loop(0, CHIPS // GROUP, gone, 0)


def pack(rows, *after):
    assert len(after) == AFTER
    shape = (CHIPS, DT, SLICE, DV)
    anywhere = pl.BlockSpec(memory_space=pl.ANY)
    return pl.pallas_call(
        pack_kernel,
        out_shape=pltpu.HBM(shape, jnp.bfloat16),
        in_specs=[anywhere] * (1 + AFTER),
        out_specs=anywhere,
        scratch_shapes=[
            pltpu.VMEM((NVT, SLICE, NVT * TILE), jnp.bfloat16),
            pltpu.VMEM((NVT, SLICE, TILE), jnp.bfloat16),
            pltpu.VMEM((OWNERS, TILE), jnp.int32),
            pltpu.SMEM((OWNERS, TILE), jnp.int32),
            pltpu.VMEM(shape, jnp.bfloat16),
            pltpu.SemaphoreType.DMA((NVT // 4,)),
            pltpu.SemaphoreType.DMA((2,)),
            pltpu.SemaphoreType.DMA((CHIPS // GROUP,)),
        ],
        compiler_params=pltpu.CompilerParams(vmem_limit_bytes=30 * MIB),
        cost_estimate=pl.CostEstimate(
            flops=0, bytes_accessed=4 * CHIPS * DT * SLICE * DV, transcendentals=0
        ),
    )(*map(in_hbm, (rows, *after)))


def cycle_kernel(
    amps_ref, exch_all_ref, exch_ref, row_ref, col_ref, after_ref, base_ref, turned_ref
):
    del after_ref
    cycle = jnp.dot(amps_ref[...], exch_all_ref[...], preferred_element_type=jnp.float32)
    cycle = cycle.astype(jnp.bfloat16).astype(jnp.float32)
    denominator = col_ref[...] + row_ref[...]
    base_ref[...] = (
        exch_ref[...].astype(jnp.float32)
        + denominator * amps_ref[...].astype(jnp.float32)
        + cycle
    )
    turned_ref[...] = cycle.T.astype(jnp.bfloat16)


def cycle_and_base(amps, exch, row, col, after):
    return pl.pallas_call(
        cycle_kernel,
        out_shape=(pltpu.HBM((DV, DV), jnp.float32), pltpu.HBM((DV, DV), jnp.bfloat16)),
        grid=(DT,),
        in_specs=[
            pl.BlockSpec((TILE, DV), lambda i: (i, 0)),
            pl.BlockSpec((DV, DV), lambda i: (0, 0)),
            pl.BlockSpec((TILE, DV), lambda i: (i, 0)),
            pl.BlockSpec((1, DV), lambda i: (0, 0)),
            pl.BlockSpec((TILE, 1), lambda i: (i, 0)),
            pl.BlockSpec(memory_space=pl.ANY),
        ],
        out_specs=(
            pl.BlockSpec((TILE, DV), lambda i: (i, 0)),
            pl.BlockSpec((DV, TILE), lambda i: (0, i)),
        ),
        compiler_params=pltpu.CompilerParams(vmem_limit_bytes=32 * MIB),
        cost_estimate=pl.CostEstimate(
            flops=2 * DV**3, bytes_accessed=14 * DV * DV, transcendentals=0
        ),
    )(amps, exch, exch, row, col, in_hbm(after))


def choose_kernel(home_ref, *refs):
    sources, targets, sems = (refs[:2], refs[2:4]), refs[4:6], refs[6]
    home = home_ref[0] > 0

    def copies(which):
        made = []
        for k in range(2):
            for i in range(DT):
                place = pl.ds(i * TILE, TILE)
                made.append(
                    pltpu.make_async_copy(
                        sources[which][k].at[place], targets[k].at[place], sems.at[k, i]
                    )
                )
        return made

    for which in range(2):

        @pl.when(home if which == 0 else jnp.logical_not(home))
        def _(which=which):
            made = copies(which)
            for copy in made:
                copy.start()
            for copy in made:
                copy.wait()


def choose(home, at_home, elsewhere):
    vmem = pl.BlockSpec(memory_space=pltpu.VMEM)
    return pl.pallas_call(
        choose_kernel,
        out_shape=[pltpu.VMEM((DV, DV), jnp.bfloat16)] * 2,
        in_specs=[pl.BlockSpec(memory_space=pltpu.SMEM)] + [pl.BlockSpec(memory_space=pl.ANY)] * 4,
        out_specs=[vmem, vmem],
        scratch_shapes=[pltpu.SemaphoreType.DMA((2, DT))],
        compiler_params=pltpu.CompilerParams(vmem_limit_bytes=8 * MIB),
        cost_estimate=pl.CostEstimate(flops=0, bytes_accessed=4 * DV * DV, transcendentals=0),
    )(home, *at_home, *elsewhere)


def ladder_kernel(raw, home, amps_ref, given_ref, added_ref, *refs):
    refs = list(refs)
    home_ref = refs.pop(0) if home else None
    refs.pop(0)
    kept_ref, sent_ref = refs.pop(0), refs.pop(0)
    rest_ref = refs.pop(0)
    block_ref = refs.pop(0) if raw else given_ref
    half, total = refs.pop(0), refs.pop(0)
    if raw:
        landed, sems = refs.pop(0), refs.pop(0)
        copies = [
            [
                pltpu.make_async_copy(given_ref.at[q, :, i], landed.at[q, i], sems.at[q, i])
                for i in range(DT)
            ]
            for q in range(NZ)
        ]
        for q in range(NZ):
            for copy in copies[q]:
                copy.start()
    for q in range(NZ):
        if raw:
            for i in range(DT):
                copies[q][i].wait()
                tile = landed[q, i].astype(jnp.float32).reshape(TILE, DV)
                block_ref[q, i * TILE : (i + 1) * TILE, :] = tile.astype(jnp.bfloat16)
        half[...] = lax.dot_general(
            amps_ref[...],
            block_ref[q],
            (((1,), (1,)), ((), ())),
            preferred_element_type=jnp.float32,
        ).astype(jnp.bfloat16)
        for i in range(DT):
            place = slice(i * TILE, (i + 1) * TILE)
            part = jnp.dot(
                block_ref[q, place, :], half[...], preferred_element_type=jnp.float32
            )
            if q > 0:
                part = part + total[place, :]
            if q < NZ - 1:
                total[place, :] = part
            else:
                if home:
                    keep = (home_ref[0] > 0).astype(jnp.float32)
                    kept_ref[place, :] = added_ref[place, :] + keep * part
                else:
                    kept_ref[place, :] = part
                    part = part + added_ref[place, :].astype(jnp.float32)
                if i < CUT:
                    sent_ref[place, :] = part.astype(jnp.bfloat16)
                else:
                    rest_ref[(i - CUT) * TILE : (i + 1 - CUT) * TILE, :] = part.astype(jnp.bfloat16)


def in_vmem(value):
    return pltpu.with_memory_space_constraint(value, pltpu.VMEM)


def ladder(amps, blocks, added, after, home=None):
    raw = blocks.ndim == 5
    vmem = pl.BlockSpec(memory_space=pltpu.VMEM)
    anywhere = pl.BlockSpec(memory_space=pl.ANY)
    scratch = [pltpu.VMEM((DV, DV), jnp.bfloat16), pltpu.VMEM((DV, DV), jnp.float32)]
    out_shape = [pltpu.VMEM((DV, DV), jnp.float32)]
    out_shape += [pltpu.VMEM((height, DV), jnp.bfloat16) for height in (CUT * TILE, DV - CUT * TILE)]
    if raw:
        out_shape.append(pltpu.VMEM((NZ, DV, DV), jnp.bfloat16))
        scratch += [
            pltpu.VMEM((NZ, DT, OWNERS, SLICE, DV), jnp.bfloat16),
            pltpu.SemaphoreType.DMA((NZ, DT)),
        ]
    operands = [in_vmem(amps), in_hbm(blocks) if raw else in_vmem(blocks), in_vmem(added)]
    specs = [vmem, anywhere if raw else vmem, vmem]
    if home is not None:
        operands.append(home)
        specs.append(pl.BlockSpec(memory_space=pltpu.SMEM))
    return pl.pallas_call(
        functools.partial(ladder_kernel, raw, home is not None),
        out_shape=out_shape,
        in_specs=specs + [anywhere],
        out_specs=[vmem] * len(out_shape),
        scratch_shapes=scratch,
        compiler_params=pltpu.CompilerParams(vmem_limit_bytes=16 * MIB),
        cost_estimate=pl.CostEstimate(
            flops=4 * NZ * DV**3, bytes_accessed=2 * NZ * DV * DV, transcendentals=0
        ),
    )(*operands, after)


def add_kernel(kept_ref, *refs):
    received, out_ref = refs[:2], refs[2]
    for i in range(DT):
        place = slice(i * TILE, (i + 1) * TILE)
        k, at = (0, i) if i < CUT else (1, i - CUT)
        came = received[k][at * TILE : (at + 1) * TILE, :].astype(jnp.float32)
        out_ref[place, :] = (kept_ref[place, :] + came).astype(jnp.bfloat16)


def add(kept, received):
    vmem = pl.BlockSpec(memory_space=pltpu.VMEM)
    return pl.pallas_call(
        add_kernel,
        out_shape=pltpu.VMEM((DV, DV), jnp.bfloat16),
        in_specs=[vmem] * 3,
        out_specs=vmem,
        compiler_params=pltpu.CompilerParams(vmem_limit_bytes=16 * MIB),
        cost_estimate=pl.CostEstimate(flops=DV * DV, bytes_accessed=DV * DV, transcendentals=0),
    )(*map(in_vmem, (kept, *received)))


def finish_kernel(kept_ref, partner_ref, returned_ref, *refs):
    received, out_ref = refs[:2], refs[2]
    for i in range(DT):
        place = slice(i * TILE, (i + 1) * TILE)
        k, at = (0, i) if i < CUT else (1, i - CUT)
        value = kept_ref[place, :] + received[k][at * TILE : (at + 1) * TILE, :].astype(jnp.float32)
        value = value + partner_ref[place, :].astype(jnp.float32)
        value = value + returned_ref[place, :].astype(jnp.float32)
        out_ref[place, :] = value.astype(jnp.bfloat16)


def finish(kept, partner_turned, returned, received):
    vmem = pl.BlockSpec(memory_space=pltpu.VMEM)
    return pl.pallas_call(
        finish_kernel,
        out_shape=jax.ShapeDtypeStruct((DV, DV), jnp.bfloat16),
        in_specs=[vmem] * 5,
        out_specs=vmem,
        compiler_params=pltpu.CompilerParams(vmem_limit_bytes=16 * MIB),
        cost_estimate=pl.CostEstimate(flops=DV * DV, bytes_accessed=DV * DV, transcendentals=0),
    )(*map(in_vmem, (kept, partner_turned, returned, *received)))


def local(amplitudes, exchange_ints, chol, domain, virt_energy, pair_energy):
    z = lax.axis_index("z")
    core = lax.axis_index("core")
    home = core == z // 2
    amps, exch = amplitudes[0], exchange_ints[0]
    column_group = ("z", "core")

    own = domain[0]
    flip_z = lambda pair: [(z * NC + c, (z ^ 1) * NC + (c ^ pair)) for z in range(NZ) for c in range(NC)]
    beside = lax.ppermute(own, column_group, flip_z(0))
    across = lax.ppermute(own, column_group, flip_z(1))
    swapped = core_swap(own)
    even, first_core = z % 2 == 0, core == 0
    mine = jnp.stack([jnp.where(even, own, beside), jnp.where(even, beside, own)])
    others = jnp.stack([jnp.where(even, swapped, across), jnp.where(even, across, swapped)])
    column = jnp.stack([jnp.where(first_core, mine, others), jnp.where(first_core, others, mine)])
    table = column.reshape(1, NZ * DT).astype(jnp.bfloat16)
    table = jnp.pad(table, ((0, SLICE - 1), (0, TILE - NZ * DT)))

    outgoing = with_table(spread(chol.reshape(2 * OWNERS, SLICE, NVT * TILE)), table)
    rows = lax.all_to_all(outgoing, ("x", "y"), 0, 0, tiled=True)
    rows = rows.reshape(NVT, SLICE, (NVT + 1) * TILE)

    early, _ = lax.optimization_barrier((amps, outgoing))
    moved = lax.ppermute(early, column_group, partner_perm(True))
    home_amps = lax.ppermute(early, column_group, home_perm(True))

    energies = jnp.take(virt_energy.reshape(NVT, TILE), own, axis=0).reshape(DV)
    base, turned = cycle_and_base(
        amps, exch, energies[None, :], (energies - pair_energy[0])[:, None], outgoing
    )

    moved, _ = lax.optimization_barrier((moved, turned))
    remote_amps = lax.ppermute(moved, column_group, home_perm(False))
    is_home = home.astype(jnp.int32)[None]
    home_amps, remote_amps = choose(is_home, (amps, remote_amps), (home_amps, moved))

    packed = pack(rows, home_amps, remote_amps, turned)
    arrived = lax.all_to_all(packed, ("z", "x", "y"), 0, 0, tiled=True)
    blocks = arrived.reshape(NZ, OWNERS, DT, SLICE, DV)

    turned_late, _ = lax.optimization_barrier((turned, arrived))
    partner_turned = lax.ppermute(turned_late, column_group, partner_perm(False))

    kept, *sent, blocks = ladder(remote_amps, blocks, turned, own)
    received = [lax.ppermute(part, column_group, home_perm(True)) for part in sent]
    kept, partner_turned = lax.optimization_barrier((kept, partner_turned))
    finished = add(kept, received)
    returned = lax.ppermute(finished, column_group, partner_perm(True))

    kept, *sent = ladder(home_amps, blocks, base, finished, is_home)
    received = [lax.ppermute(part, column_group, home_perm(False)) for part in sent]
    return finish(kept, partner_turned, returned, received)[None]


def solution(mesh):
    finer = Mesh(mesh.devices.reshape(NZ, NC, NX, NY), ("z", "core", "x", "y"))
    group, everywhere = ("z", "core"), ("z", "core", "x", "y")
    placed = (
        P(everywhere, None, None),
        P(everywhere, None, None),
        P(group, ("x", "y"), None),
        P(everywhere, None),
        P(),
        P(everywhere),
    )
    return jax.shard_map(
        local, mesh=finer, in_specs=placed, out_specs=P(everywhere, None, None), check_vma=False
    )
```

```python
import functools

import jax
import jax.numpy as jnp
from jax import lax
from jax.experimental import pallas as pl
from jax.experimental.pallas import tpu as pltpu
from jax.sharding import Mesh
from jax.sharding import PartitionSpec as P

TILE = 128
NVT = 32
DT = 7
DV = DT * TILE
NZ, NC, NX, NY = 4, 2, 4, 4
OWNERS = NX * NY
SLICE = TILE // OWNERS
CHIPS = NZ * OWNERS
AFTER = 3
CUT = 4
BEGIN = 1
GROUP = 4
MIB = 1024 * 1024


def partner_perm(to_other_core):
    pairs = []
    for z in range(NZ):
        core = 1 - z // 2
        target = 1 - core if to_other_core else core
        pairs.append((z * NC + core, (z ^ 2) * NC + target))
    return pairs


def home_perm(from_home):
    pairs = [(z * NC + z // 2, z * NC + 1 - z // 2) for z in range(NZ)]
    return pairs if from_home else [(b, a) for a, b in pairs]


def core_swap(value):
    return lax.ppermute(value, "core", [(0, 1), (1, 0)])


def in_hbm(value):
    return pltpu.with_memory_space_constraint(value, pltpu.HBM)


def spread_kernel(chol_ref, out_ref, staged, in_sems, out_sems):
    arriving, leaving = [], []
    for m in range(OWNERS):
        for t in range(2):
            place = (m, t, slice(None), slice(0, NVT * TILE))
            arriving.append(
                pltpu.make_async_copy(
                    chol_ref.at[t * OWNERS + m], staged.at[m, t], in_sems.at[m, t]
                )
            )
            leaving.append(
                pltpu.make_async_copy(staged.at[m, t], out_ref.at[place], out_sems.at[m, t])
            )
    for copy in arriving:
        copy.start()
    for come, leave in zip(arriving, leaving):
        come.wait()
        leave.start()
    for copy in leaving:
        copy.wait()


def spread(chol):
    return pl.pallas_call(
        spread_kernel,
        out_shape=pltpu.HBM((OWNERS, 2, SLICE, (NVT + 1) * TILE), jnp.bfloat16),
        in_specs=[pl.BlockSpec(memory_space=pl.ANY)],
        out_specs=pl.BlockSpec(memory_space=pl.ANY),
        scratch_shapes=[
            pltpu.VMEM((OWNERS, 2, SLICE, NVT * TILE), jnp.bfloat16),
            pltpu.SemaphoreType.DMA((OWNERS, 2)),
            pltpu.SemaphoreType.DMA((OWNERS, 2)),
        ],
        compiler_params=pltpu.CompilerParams(vmem_limit_bytes=30 * MIB),
        cost_estimate=pl.CostEstimate(flops=0, bytes_accessed=4 * MIB, transcendentals=0),
    )(in_hbm(chol))


def table_kernel(table_ref, given_ref, out_ref, sems):
    del given_ref
    copies = []
    for m in range(OWNERS):
        for t in range(2):
            copies.append(
                pltpu.make_async_copy(
                    table_ref, out_ref.at[m, t, :, pl.ds(NVT * TILE, TILE)], sems.at[m, t]
                )
            )
    for copy in copies:
        copy.start()
    for copy in copies:
        copy.wait()


def with_table(spread_rows, table):
    anywhere = pl.BlockSpec(memory_space=pl.ANY)
    return pl.pallas_call(
        table_kernel,
        out_shape=pltpu.HBM(spread_rows.shape, jnp.bfloat16),
        in_specs=[pl.BlockSpec(memory_space=pltpu.VMEM), anywhere],
        out_specs=anywhere,
        scratch_shapes=[pltpu.SemaphoreType.DMA((OWNERS, 2))],
        input_output_aliases={1: 0},
        compiler_params=pltpu.CompilerParams(vmem_limit_bytes=8 * MIB),
    )(table, in_hbm(spread_rows))


def pack_kernel(given_ref, *refs):
    out_ref, rows_ref, given_tables, tables, tiles_ref, packed, row_sems, table_sems, sems = refs[AFTER:]
    beside = pltpu.make_async_copy(
        given_ref.at[:, :, pl.ds(NVT * TILE, TILE)], given_tables, table_sems.at[0]
    )
    beside.start()
    fetches = []
    for k in range(NVT // 4):
        part = pl.ds(k * 4, 4)
        fetches.append(
            pltpu.make_async_copy(
                given_ref.at[part, :, pl.ds(0, NVT * TILE)], rows_ref.at[part], row_sems.at[k]
            )
        )
    for fetch in fetches:
        fetch.start()
    beside.wait()
    for s in range(OWNERS):
        table = given_tables[2 * s].astype(jnp.float32).astype(jnp.int32)
        tables[s : s + 1, :] = table[0:1, :]
    move = pltpu.make_async_copy(tables, tiles_ref, table_sems.at[1])
    move.start()
    move.wait()
    for fetch in fetches:
        fetch.wait()

    def leave(group):
        dests = pl.ds(group * GROUP, GROUP)
        return pltpu.make_async_copy(packed.at[dests], out_ref.at[dests], sems.at[group])

    def one(group, carry):
        for k in range(GROUP):
            dest = group * GROUP + k
            z, s = dest // OWNERS, dest % OWNERS
            tiles = [tiles_ref[s, z * DT + t] for t in range(DT)]
            columns = [pl.multiple_of(tile * TILE, TILE) for tile in tiles]
            for i in range(DT):
                for j in range(DT):
                    packed[dest, i, :, j * TILE : (j + 1) * TILE] = rows_ref[
                        tiles[i], :, pl.ds(columns[j], TILE)
                    ]
        leave(group).start()
        return carry

    def gone(group, carry):
        leave(group).wait()
        return carry

    lax.fori_loop(0, CHIPS // GROUP, one, 0)
    lax.fori_loop(0, CHIPS // GROUP, gone, 0)


def pack(rows, *after):
    assert len(after) == AFTER
    shape = (CHIPS, DT, SLICE, DV)
    anywhere = pl.BlockSpec(memory_space=pl.ANY)
    return pl.pallas_call(
        pack_kernel,
        out_shape=pltpu.HBM(shape, jnp.bfloat16),
        in_specs=[anywhere] * (1 + AFTER),
        out_specs=anywhere,
        scratch_shapes=[
            pltpu.VMEM((NVT, SLICE, NVT * TILE), jnp.bfloat16),
            pltpu.VMEM((NVT, SLICE, TILE), jnp.bfloat16),
            pltpu.VMEM((OWNERS, TILE), jnp.int32),
            pltpu.SMEM((OWNERS, TILE), jnp.int32),
            pltpu.VMEM(shape, jnp.bfloat16),
            pltpu.SemaphoreType.DMA((NVT // 4,)),
            pltpu.SemaphoreType.DMA((2,)),
            pltpu.SemaphoreType.DMA((CHIPS // GROUP,)),
        ],
        compiler_params=pltpu.CompilerParams(vmem_limit_bytes=30 * MIB),
        cost_estimate=pl.CostEstimate(
            flops=0, bytes_accessed=4 * CHIPS * DT * SLICE * DV, transcendentals=0
        ),
    )(*map(in_hbm, (rows, *after)))


def cycle_kernel(
    amps_ref, exch_all_ref, exch_ref, row_ref, col_ref, after_ref, base_ref, turned_ref
):
    del after_ref
    cycle = jnp.dot(amps_ref[...], exch_all_ref[...], preferred_element_type=jnp.float32)
    cycle = cycle.astype(jnp.bfloat16).astype(jnp.float32)
    denominator = col_ref[...] + row_ref[...]
    base_ref[...] = (
        exch_ref[...].astype(jnp.float32)
        + denominator * amps_ref[...].astype(jnp.float32)
        + cycle
    )
    turned_ref[...] = cycle.T.astype(jnp.bfloat16)


def cycle_and_base(amps, exch, row, col, after):
    return pl.pallas_call(
        cycle_kernel,
        out_shape=(pltpu.HBM((DV, DV), jnp.float32), pltpu.HBM((DV, DV), jnp.bfloat16)),
        grid=(DT,),
        in_specs=[
            pl.BlockSpec((TILE, DV), lambda i: (i, 0)),
            pl.BlockSpec((DV, DV), lambda i: (0, 0)),
            pl.BlockSpec((TILE, DV), lambda i: (i, 0)),
            pl.BlockSpec((1, DV), lambda i: (0, 0)),
            pl.BlockSpec((TILE, 1), lambda i: (i, 0)),
            pl.BlockSpec(memory_space=pl.ANY),
        ],
        out_specs=(
            pl.BlockSpec((TILE, DV), lambda i: (i, 0)),
            pl.BlockSpec((DV, TILE), lambda i: (0, i)),
        ),
        compiler_params=pltpu.CompilerParams(vmem_limit_bytes=32 * MIB),
        cost_estimate=pl.CostEstimate(
            flops=2 * DV**3, bytes_accessed=14 * DV * DV, transcendentals=0
        ),
    )(amps, exch, exch, row, col, in_hbm(after))


def choose_kernel(home_ref, *refs):
    sources, targets, sems = (refs[:2], refs[2:4]), refs[4:6], refs[6]
    home = home_ref[0] > 0

    def copies(which):
        made = []
        for k in range(2):
            for i in range(DT):
                place = pl.ds(i * TILE, TILE)
                made.append(
                    pltpu.make_async_copy(
                        sources[which][k].at[place], targets[k].at[place], sems.at[k, i]
                    )
                )
        return made

    for which in range(2):

        @pl.when(home if which == 0 else jnp.logical_not(home))
        def _(which=which):
            made = copies(which)
            for copy in made:
                copy.start()
            for copy in made:
                copy.wait()


def choose(home, at_home, elsewhere):
    vmem = pl.BlockSpec(memory_space=pltpu.VMEM)
    return pl.pallas_call(
        choose_kernel,
        out_shape=[pltpu.VMEM((DV, DV), jnp.bfloat16)] * 2,
        in_specs=[pl.BlockSpec(memory_space=pltpu.SMEM)] + [pl.BlockSpec(memory_space=pl.ANY)] * 4,
        out_specs=[vmem, vmem],
        scratch_shapes=[pltpu.SemaphoreType.DMA((2, DT))],
        compiler_params=pltpu.CompilerParams(vmem_limit_bytes=8 * MIB),
        cost_estimate=pl.CostEstimate(flops=0, bytes_accessed=4 * DV * DV, transcendentals=0),
    )(home, *at_home, *elsewhere)


def ladder_products(vectors, amps_ref, block_ref, half, total, so_far, ready, give):
    ready(vectors[0])
    for q in vectors:
        half[...] = lax.dot_general(
            amps_ref[...],
            block_ref[q],
            (((1,), (1,)), ((), ())),
            preferred_element_type=jnp.float32,
        ).astype(jnp.bfloat16)
        if q < vectors[-1]:
            ready(q + 1)
        for i in range(DT):
            place = slice(i * TILE, (i + 1) * TILE)
            part = jnp.dot(
                block_ref[q, place, :], half[...], preferred_element_type=jnp.float32
            )
            if q > vectors[0]:
                part = part + total[place, :]
            elif so_far is not None:
                part = part + so_far[place, :]
            if q < vectors[-1]:
                total[place, :] = part
            else:
                give(i, place, part)


def put(part, i, first_ref, second_ref):
    target, at = (first_ref, i) if i < CUT else (second_ref, i - CUT)
    target[at * TILE : (at + 1) * TILE, :] = part.astype(jnp.bfloat16)


def remote_kernel(amps_ref, given_ref, added_ref, *refs):
    kept_ref, sent_ref, block_ref, half, total, landed, sems = refs
    copies = [
        [
            pltpu.make_async_copy(given_ref.at[q, :, i], landed.at[q, i], sems.at[q, i])
            for i in range(DT)
        ]
        for q in range(NZ)
    ]
    for q in range(NZ):
        for copy in copies[q]:
            copy.start()

    def ready(q):
        for copy in copies[q]:
            copy.wait()
        for i in range(DT):
            tile = landed[q, i].astype(jnp.float32).reshape(TILE, DV)
            block_ref[q, i * TILE : (i + 1) * TILE, :] = tile.astype(jnp.bfloat16)

    def give(i, place, part):
        kept_ref[place, :] = part
        sent_ref[place, :] = (part + added_ref[place, :].astype(jnp.float32)).astype(jnp.bfloat16)

    ladder_products(range(NZ), amps_ref, block_ref, half, total, None, ready, give)


def begin_kernel(amps_ref, block_ref, total_ref, half):
    def give(i, place, part):
        total_ref[place, :] = part

    ladder_products(range(BEGIN), amps_ref, block_ref, half, total_ref, None, lambda q: None, give)


def home_kernel(home_ref, amps_ref, block_ref, so_far_ref, added_ref, after_ref, *refs):
    del after_ref
    kept_ref, first_ref, second_ref, half, total = refs
    keep = (home_ref[0] > 0).astype(jnp.float32)

    def give(i, place, part):
        kept_ref[place, :] = added_ref[place, :] + keep * part
        put(part, i, first_ref, second_ref)

    ladder_products(
        range(BEGIN, NZ), amps_ref, block_ref, half, total, so_far_ref, lambda q: None, give
    )


def in_vmem(value):
    return pltpu.with_memory_space_constraint(value, pltpu.VMEM)


def ladder_cost(vectors):
    return pl.CostEstimate(
        flops=4 * vectors * DV**3, bytes_accessed=2 * vectors * DV * DV, transcendentals=0
    )


def remote_ladder(amps, arrived, turned):
    vmem, anywhere = pl.BlockSpec(memory_space=pltpu.VMEM), pl.BlockSpec(memory_space=pl.ANY)
    out_shape = [
        pltpu.VMEM((DV, DV), jnp.float32),
        pltpu.VMEM((DV, DV), jnp.bfloat16),
        pltpu.VMEM((NZ, DV, DV), jnp.bfloat16),
    ]
    return pl.pallas_call(
        remote_kernel,
        out_shape=out_shape,
        in_specs=[vmem, anywhere, vmem],
        out_specs=[vmem] * len(out_shape),
        scratch_shapes=[
            pltpu.VMEM((DV, DV), jnp.bfloat16),
            pltpu.VMEM((DV, DV), jnp.float32),
            pltpu.VMEM((NZ, DT, OWNERS, SLICE, DV), jnp.bfloat16),
            pltpu.SemaphoreType.DMA((NZ, DT)),
        ],
        compiler_params=pltpu.CompilerParams(vmem_limit_bytes=16 * MIB),
        cost_estimate=ladder_cost(NZ),
    )(in_vmem(amps), in_hbm(arrived), in_vmem(turned))


def begin_ladder(amps, blocks):
    vmem = pl.BlockSpec(memory_space=pltpu.VMEM)
    return pl.pallas_call(
        begin_kernel,
        out_shape=pltpu.VMEM((DV, DV), jnp.float32),
        in_specs=[vmem] * 2,
        out_specs=vmem,
        scratch_shapes=[pltpu.VMEM((DV, DV), jnp.bfloat16)],
        compiler_params=pltpu.CompilerParams(vmem_limit_bytes=16 * MIB),
        cost_estimate=ladder_cost(BEGIN),
    )(in_vmem(amps), in_vmem(blocks))


def home_ladder(home, amps, blocks, so_far, base, after):
    vmem, anywhere = pl.BlockSpec(memory_space=pltpu.VMEM), pl.BlockSpec(memory_space=pl.ANY)
    out_shape = [
        pltpu.VMEM((DV, DV), jnp.float32),
        pltpu.VMEM((CUT * TILE, DV), jnp.bfloat16),
        pltpu.VMEM((DV - CUT * TILE, DV), jnp.bfloat16),
    ]
    return pl.pallas_call(
        home_kernel,
        out_shape=out_shape,
        in_specs=[pl.BlockSpec(memory_space=pltpu.SMEM)] + [vmem] * 4 + [anywhere],
        out_specs=[vmem] * len(out_shape),
        scratch_shapes=[pltpu.VMEM((DV, DV), jnp.bfloat16), pltpu.VMEM((DV, DV), jnp.float32)],
        compiler_params=pltpu.CompilerParams(vmem_limit_bytes=16 * MIB),
        cost_estimate=ladder_cost(NZ - BEGIN),
    )(home, *map(in_vmem, (amps, blocks, so_far, base)), after)


def finish_kernel(kept_ref, partner_ref, returned_ref, *refs):
    received, out_ref = refs[:2], refs[2]
    for i in range(DT):
        place = slice(i * TILE, (i + 1) * TILE)
        k, at = (0, i) if i < CUT else (1, i - CUT)
        value = kept_ref[place, :] + received[k][at * TILE : (at + 1) * TILE, :].astype(jnp.float32)
        value = value + partner_ref[place, :].astype(jnp.float32)
        value = value + returned_ref[place, :].astype(jnp.float32)
        out_ref[place, :] = value.astype(jnp.bfloat16)


def finish(kept, partner_turned, returned, received):
    vmem = pl.BlockSpec(memory_space=pltpu.VMEM)
    return pl.pallas_call(
        finish_kernel,
        out_shape=jax.ShapeDtypeStruct((DV, DV), jnp.bfloat16),
        in_specs=[vmem] * 5,
        out_specs=vmem,
        compiler_params=pltpu.CompilerParams(vmem_limit_bytes=16 * MIB),
        cost_estimate=pl.CostEstimate(flops=DV * DV, bytes_accessed=DV * DV, transcendentals=0),
    )(*map(in_vmem, (kept, partner_turned, returned, *received)))


def local(amplitudes, exchange_ints, chol, domain, virt_energy, pair_energy):
    z = lax.axis_index("z")
    core = lax.axis_index("core")
    home = core == z // 2
    amps, exch = amplitudes[0], exchange_ints[0]
    column_group = ("z", "core")

    own = domain[0]
    flip_z = lambda pair: [(z * NC + c, (z ^ 1) * NC + (c ^ pair)) for z in range(NZ) for c in range(NC)]
    beside = lax.ppermute(own, column_group, flip_z(0))
    across = lax.ppermute(own, column_group, flip_z(1))
    swapped = core_swap(own)
    even, first_core = z % 2 == 0, core == 0
    mine = jnp.stack([jnp.where(even, own, beside), jnp.where(even, beside, own)])
    others = jnp.stack([jnp.where(even, swapped, across), jnp.where(even, across, swapped)])
    column = jnp.stack([jnp.where(first_core, mine, others), jnp.where(first_core, others, mine)])
    table = column.reshape(1, NZ * DT).astype(jnp.bfloat16)
    table = jnp.pad(table, ((0, SLICE - 1), (0, TILE - NZ * DT)))

    outgoing = with_table(spread(chol.reshape(2 * OWNERS, SLICE, NVT * TILE)), table)
    rows = lax.all_to_all(outgoing, ("x", "y"), 0, 0, tiled=True)
    rows = rows.reshape(NVT, SLICE, (NVT + 1) * TILE)

    early, _ = lax.optimization_barrier((amps, outgoing))
    moved = lax.ppermute(early, column_group, partner_perm(True))
    home_amps = lax.ppermute(early, column_group, home_perm(True))

    energies = jnp.take(virt_energy.reshape(NVT, TILE), own, axis=0).reshape(DV)
    base, turned = cycle_and_base(
        amps, exch, energies[None, :], (energies - pair_energy[0])[:, None], outgoing
    )

    moved, _ = lax.optimization_barrier((moved, turned))
    remote_amps = lax.ppermute(moved, column_group, home_perm(False))
    is_home = home.astype(jnp.int32)[None]
    home_amps, remote_amps = choose(is_home, (amps, remote_amps), (home_amps, moved))

    packed = pack(rows, home_amps, remote_amps, turned)
    arrived = lax.all_to_all(packed, ("z", "x", "y"), 0, 0, tiled=True)
    arrived = arrived.reshape(NZ, OWNERS, DT, SLICE, DV)

    turned_late, _ = lax.optimization_barrier((turned, arrived))
    partner_turned = lax.ppermute(turned_late, column_group, partner_perm(False))

    kept, sent, blocks = remote_ladder(remote_amps, arrived, turned)
    received = lax.ppermute(sent, column_group, home_perm(True))
    home_amps, partner_turned = lax.optimization_barrier((home_amps, partner_turned))
    begun = begin_ladder(home_amps, blocks)
    kept, begun = lax.optimization_barrier((kept, begun))
    finished = (kept + received.astype(jnp.float32)).astype(jnp.bfloat16)
    returned = lax.ppermute(finished, column_group, partner_perm(True))

    kept, *sent = home_ladder(is_home, home_amps, blocks, begun, base, finished)
    received = [lax.ppermute(part, column_group, home_perm(False)) for part in sent]
    return finish(kept, partner_turned, returned, received)[None]


def solution(mesh):
    finer = Mesh(mesh.devices.reshape(NZ, NC, NX, NY), ("z", "core", "x", "y"))
    group, everywhere = ("z", "core"), ("z", "core", "x", "y")
    placed = (
        P(everywhere, None, None),
        P(everywhere, None, None),
        P(group, ("x", "y"), None),
        P(everywhere, None),
        P(),
        P(everywhere),
    )
    return jax.shard_map(
        local, mesh=finer, in_specs=placed, out_specs=P(everywhere, None, None), check_vma=False
    )
```

```python
import functools

import jax
import jax.numpy as jnp
from jax import lax
from jax.experimental import pallas as pl
from jax.experimental.pallas import tpu as pltpu
from jax.sharding import Mesh
from jax.sharding import PartitionSpec as P

TILE = 128
NVT = 32
DT = 7
DV = DT * TILE
NZ, NC, NX, NY = 4, 2, 4, 4
OWNERS = NX * NY
SLICE = TILE // OWNERS
CHIPS = NZ * OWNERS
AFTER = 3
CUT = 4
BEGIN = 1
GROUP = 4
MIB = 1024 * 1024


def partner_perm(to_other_core):
    pairs = []
    for z in range(NZ):
        core = 1 - z // 2
        target = 1 - core if to_other_core else core
        pairs.append((z * NC + core, (z ^ 2) * NC + target))
    return pairs


def home_perm(from_home):
    pairs = [(z * NC + z // 2, z * NC + 1 - z // 2) for z in range(NZ)]
    return pairs if from_home else [(b, a) for a, b in pairs]


def core_swap(value):
    return lax.ppermute(value, "core", [(0, 1), (1, 0)])


def in_hbm(value):
    return pltpu.with_memory_space_constraint(value, pltpu.HBM)


def spread_kernel(chol_ref, out_ref, staged, in_sems, out_sems):
    arriving, leaving = [], []
    for m in range(OWNERS):
        for t in range(2):
            place = (m, t, slice(None), slice(0, NVT * TILE))
            arriving.append(
                pltpu.make_async_copy(
                    chol_ref.at[t * OWNERS + m], staged.at[m, t], in_sems.at[m, t]
                )
            )
            leaving.append(
                pltpu.make_async_copy(staged.at[m, t], out_ref.at[place], out_sems.at[m, t])
            )
    for copy in arriving:
        copy.start()
    for come, leave in zip(arriving, leaving):
        come.wait()
        leave.start()
    for copy in leaving:
        copy.wait()


def spread(chol):
    return pl.pallas_call(
        spread_kernel,
        out_shape=pltpu.HBM((OWNERS, 2, SLICE, (NVT + 1) * TILE), jnp.bfloat16),
        in_specs=[pl.BlockSpec(memory_space=pl.ANY)],
        out_specs=pl.BlockSpec(memory_space=pl.ANY),
        scratch_shapes=[
            pltpu.VMEM((OWNERS, 2, SLICE, NVT * TILE), jnp.bfloat16),
            pltpu.SemaphoreType.DMA((OWNERS, 2)),
            pltpu.SemaphoreType.DMA((OWNERS, 2)),
        ],
        compiler_params=pltpu.CompilerParams(vmem_limit_bytes=30 * MIB),
        cost_estimate=pl.CostEstimate(flops=0, bytes_accessed=4 * MIB, transcendentals=0),
    )(in_hbm(chol))


def table_kernel(table_ref, given_ref, out_ref, sems):
    del given_ref
    copies = []
    for m in range(OWNERS):
        for t in range(2):
            copies.append(
                pltpu.make_async_copy(
                    table_ref, out_ref.at[m, t, :, pl.ds(NVT * TILE, TILE)], sems.at[m, t]
                )
            )
    for copy in copies:
        copy.start()
    for copy in copies:
        copy.wait()


def with_table(spread_rows, table):
    anywhere = pl.BlockSpec(memory_space=pl.ANY)
    return pl.pallas_call(
        table_kernel,
        out_shape=pltpu.HBM(spread_rows.shape, jnp.bfloat16),
        in_specs=[pl.BlockSpec(memory_space=pltpu.VMEM), anywhere],
        out_specs=anywhere,
        scratch_shapes=[pltpu.SemaphoreType.DMA((OWNERS, 2))],
        input_output_aliases={1: 0},
        compiler_params=pltpu.CompilerParams(vmem_limit_bytes=8 * MIB),
    )(table, in_hbm(spread_rows))


def pack_kernel(given_ref, *refs):
    out_ref, rows_ref, given_tables, tables, tiles_ref, packed, row_sems, table_sems, sems = refs[AFTER:]
    beside = pltpu.make_async_copy(
        given_ref.at[:, :, pl.ds(NVT * TILE, TILE)], given_tables, table_sems.at[0]
    )
    beside.start()
    fetches = []
    for k in range(NVT // 4):
        part = pl.ds(k * 4, 4)
        fetches.append(
            pltpu.make_async_copy(
                given_ref.at[part, :, pl.ds(0, NVT * TILE)], rows_ref.at[part], row_sems.at[k]
            )
        )
    for fetch in fetches:
        fetch.start()
    beside.wait()
    for s in range(OWNERS):
        table = given_tables[2 * s].astype(jnp.float32).astype(jnp.int32)
        tables[s : s + 1, :] = table[0:1, :]
    move = pltpu.make_async_copy(tables, tiles_ref, table_sems.at[1])
    move.start()
    move.wait()
    for fetch in fetches:
        fetch.wait()

    def leave(group):
        dests = pl.ds(group * GROUP, GROUP)
        return pltpu.make_async_copy(packed.at[dests], out_ref.at[dests], sems.at[group])

    def one(group, carry):
        for k in range(GROUP):
            dest = group * GROUP + k
            z, s = dest // OWNERS, dest % OWNERS
            tiles = [tiles_ref[s, z * DT + t] for t in range(DT)]
            columns = [pl.multiple_of(tile * TILE, TILE) for tile in tiles]
            for i in range(DT):
                for j in range(DT):
                    packed[dest, i, :, j * TILE : (j + 1) * TILE] = rows_ref[
                        tiles[i], :, pl.ds(columns[j], TILE)
                    ]
        leave(group).start()
        return carry

    def gone(group, carry):
        leave(group).wait()
        return carry

    lax.fori_loop(0, CHIPS // GROUP, one, 0)
    lax.fori_loop(0, CHIPS // GROUP, gone, 0)


def pack(rows, *after):
    assert len(after) == AFTER
    shape = (CHIPS, DT, SLICE, DV)
    anywhere = pl.BlockSpec(memory_space=pl.ANY)
    return pl.pallas_call(
        pack_kernel,
        out_shape=pltpu.HBM(shape, jnp.bfloat16),
        in_specs=[anywhere] * (1 + AFTER),
        out_specs=anywhere,
        scratch_shapes=[
            pltpu.VMEM((NVT, SLICE, NVT * TILE), jnp.bfloat16),
            pltpu.VMEM((NVT, SLICE, TILE), jnp.bfloat16),
            pltpu.VMEM((OWNERS, TILE), jnp.int32),
            pltpu.SMEM((OWNERS, TILE), jnp.int32),
            pltpu.VMEM(shape, jnp.bfloat16),
            pltpu.SemaphoreType.DMA((NVT // 4,)),
            pltpu.SemaphoreType.DMA((2,)),
            pltpu.SemaphoreType.DMA((CHIPS // GROUP,)),
        ],
        compiler_params=pltpu.CompilerParams(vmem_limit_bytes=30 * MIB),
        cost_estimate=pl.CostEstimate(
            flops=0, bytes_accessed=4 * CHIPS * DT * SLICE * DV, transcendentals=0
        ),
    )(*map(in_hbm, (rows, *after)))


def cycle_kernel(
    amps_ref, exch_all_ref, exch_ref, row_ref, col_ref, after_ref, base_ref, turned_ref
):
    del after_ref
    cycle = jnp.dot(amps_ref[...], exch_all_ref[...], preferred_element_type=jnp.float32)
    cycle = cycle.astype(jnp.bfloat16).astype(jnp.float32)
    denominator = col_ref[...] + row_ref[...]
    base_ref[...] = (
        exch_ref[...].astype(jnp.float32)
        + denominator * amps_ref[...].astype(jnp.float32)
        + cycle
    )
    turned_ref[...] = cycle.T.astype(jnp.bfloat16)


def cycle_and_base(amps, exch, row, col, after):
    return pl.pallas_call(
        cycle_kernel,
        out_shape=(pltpu.HBM((DV, DV), jnp.float32), pltpu.HBM((DV, DV), jnp.bfloat16)),
        grid=(DT,),
        in_specs=[
            pl.BlockSpec((TILE, DV), lambda i: (i, 0)),
            pl.BlockSpec((DV, DV), lambda i: (0, 0)),
            pl.BlockSpec((TILE, DV), lambda i: (i, 0)),
            pl.BlockSpec((1, DV), lambda i: (0, 0)),
            pl.BlockSpec((TILE, 1), lambda i: (i, 0)),
            pl.BlockSpec(memory_space=pl.ANY),
        ],
        out_specs=(
            pl.BlockSpec((TILE, DV), lambda i: (i, 0)),
            pl.BlockSpec((DV, TILE), lambda i: (0, i)),
        ),
        compiler_params=pltpu.CompilerParams(vmem_limit_bytes=32 * MIB),
        cost_estimate=pl.CostEstimate(
            flops=2 * DV**3, bytes_accessed=14 * DV * DV, transcendentals=0
        ),
    )(amps, exch, exch, row, col, in_hbm(after))


def choose_kernel(home_ref, *refs):
    sources, targets, sems = (refs[:2], refs[2:4]), refs[4:6], refs[6]
    home = home_ref[0] > 0

    def copies(which):
        made = []
        for k in range(2):
            for i in range(DT):
                place = pl.ds(i * TILE, TILE)
                made.append(
                    pltpu.make_async_copy(
                        sources[which][k].at[place], targets[k].at[place], sems.at[k, i]
                    )
                )
        return made

    for which in range(2):

        @pl.when(home if which == 0 else jnp.logical_not(home))
        def _(which=which):
            made = copies(which)
            for copy in made:
                copy.start()
            for copy in made:
                copy.wait()


def choose(home, at_home, elsewhere):
    vmem = pl.BlockSpec(memory_space=pltpu.VMEM)
    return pl.pallas_call(
        choose_kernel,
        out_shape=[pltpu.VMEM((DV, DV), jnp.bfloat16)] * 2,
        in_specs=[pl.BlockSpec(memory_space=pltpu.SMEM)] + [pl.BlockSpec(memory_space=pl.ANY)] * 4,
        out_specs=[vmem, vmem],
        scratch_shapes=[pltpu.SemaphoreType.DMA((2, DT))],
        compiler_params=pltpu.CompilerParams(vmem_limit_bytes=8 * MIB),
        cost_estimate=pl.CostEstimate(flops=0, bytes_accessed=4 * DV * DV, transcendentals=0),
    )(home, *at_home, *elsewhere)


def ladder_products(vectors, amps_ref, block_ref, half, total, so_far, ready, give):
    ready(vectors[0])
    for q in vectors:
        half[...] = lax.dot_general(
            amps_ref[...],
            block_ref[q],
            (((1,), (1,)), ((), ())),
            preferred_element_type=jnp.float32,
        ).astype(jnp.bfloat16)
        if q < vectors[-1]:
            ready(q + 1)
        for i, (start, stop) in enumerate(((0, CUT), (CUT, DT))):
            place = slice(start * TILE, stop * TILE)
            part = jnp.dot(
                block_ref[q, place, :], half[...], preferred_element_type=jnp.float32
            )
            if q > vectors[0]:
                part = part + total[place, :]
            elif so_far is not None:
                part = part + so_far[place, :]
            if q < vectors[-1]:
                total[place, :] = part
            else:
                give(i, place, part)


def put(part, i, first_ref, second_ref):
    target = first_ref if i == 0 else second_ref
    target[...] = part.astype(jnp.bfloat16)


def remote_kernel(amps_ref, given_ref, added_ref, *refs):
    kept_ref, sent_ref, block_ref, half, total, landed, sems = refs
    copies = [
        [
            pltpu.make_async_copy(given_ref.at[q, :, i], landed.at[q, i], sems.at[q, i])
            for i in range(DT)
        ]
        for q in range(NZ)
    ]
    for q in range(NZ):
        for copy in copies[q]:
            copy.start()

    def ready(q):
        for copy in copies[q]:
            copy.wait()
        for i in range(DT):
            tile = landed[q, i].astype(jnp.float32).reshape(TILE, DV)
            block_ref[q, i * TILE : (i + 1) * TILE, :] = tile.astype(jnp.bfloat16)

    def give(i, place, part):
        kept_ref[place, :] = part
        sent_ref[place, :] = (part + added_ref[place, :].astype(jnp.float32)).astype(jnp.bfloat16)

    ladder_products(range(NZ), amps_ref, block_ref, half, total, None, ready, give)


def begin_kernel(amps_ref, block_ref, total_ref, half):
    def give(i, place, part):
        total_ref[place, :] = part

    ladder_products(range(BEGIN), amps_ref, block_ref, half, total_ref, None, lambda q: None, give)


def home_kernel(home_ref, amps_ref, block_ref, so_far_ref, added_ref, after_ref, *refs):
    del after_ref
    kept_ref, first_ref, second_ref, half, total = refs
    keep = (home_ref[0] > 0).astype(jnp.float32)

    def give(i, place, part):
        kept_ref[place, :] = added_ref[place, :] + keep * part
        put(part, i, first_ref, second_ref)

    ladder_products(
        range(BEGIN, NZ), amps_ref, block_ref, half, total, so_far_ref, lambda q: None, give
    )


def in_vmem(value):
    return pltpu.with_memory_space_constraint(value, pltpu.VMEM)


def ladder_cost(vectors):
    return pl.CostEstimate(
        flops=4 * vectors * DV**3, bytes_accessed=2 * vectors * DV * DV, transcendentals=0
    )


def remote_ladder(amps, arrived, turned):
    vmem, anywhere = pl.BlockSpec(memory_space=pltpu.VMEM), pl.BlockSpec(memory_space=pl.ANY)
    out_shape = [
        pltpu.VMEM((DV, DV), jnp.float32),
        pltpu.VMEM((DV, DV), jnp.bfloat16),
        pltpu.VMEM((NZ, DV, DV), jnp.bfloat16),
    ]
    return pl.pallas_call(
        remote_kernel,
        out_shape=out_shape,
        in_specs=[vmem, anywhere, vmem],
        out_specs=[vmem] * len(out_shape),
        scratch_shapes=[
            pltpu.VMEM((DV, DV), jnp.bfloat16),
            pltpu.VMEM((DV, DV), jnp.float32),
            pltpu.VMEM((NZ, DT, OWNERS, SLICE, DV), jnp.bfloat16),
            pltpu.SemaphoreType.DMA((NZ, DT)),
        ],
        compiler_params=pltpu.CompilerParams(vmem_limit_bytes=20 * MIB),
        cost_estimate=ladder_cost(NZ),
    )(in_vmem(amps), in_hbm(arrived), in_vmem(turned))


def begin_ladder(amps, blocks):
    vmem = pl.BlockSpec(memory_space=pltpu.VMEM)
    return pl.pallas_call(
        begin_kernel,
        out_shape=pltpu.VMEM((DV, DV), jnp.float32),
        in_specs=[vmem] * 2,
        out_specs=vmem,
        scratch_shapes=[pltpu.VMEM((DV, DV), jnp.bfloat16)],
        compiler_params=pltpu.CompilerParams(vmem_limit_bytes=20 * MIB),
        cost_estimate=ladder_cost(BEGIN),
    )(in_vmem(amps), in_vmem(blocks))


def home_ladder(home, amps, blocks, so_far, base, after):
    vmem, anywhere = pl.BlockSpec(memory_space=pltpu.VMEM), pl.BlockSpec(memory_space=pl.ANY)
    out_shape = [
        pltpu.VMEM((DV, DV), jnp.float32),
        pltpu.VMEM((CUT * TILE, DV), jnp.bfloat16),
        pltpu.VMEM((DV - CUT * TILE, DV), jnp.bfloat16),
    ]
    return pl.pallas_call(
        home_kernel,
        out_shape=out_shape,
        in_specs=[pl.BlockSpec(memory_space=pltpu.SMEM)] + [vmem] * 4 + [anywhere],
        out_specs=[vmem] * len(out_shape),
        scratch_shapes=[pltpu.VMEM((DV, DV), jnp.bfloat16), pltpu.VMEM((DV, DV), jnp.float32)],
        compiler_params=pltpu.CompilerParams(vmem_limit_bytes=20 * MIB),
        cost_estimate=ladder_cost(NZ - BEGIN),
    )(home, *map(in_vmem, (amps, blocks, so_far, base)), after)


def finish_kernel(kept_ref, partner_ref, returned_ref, *refs):
    received, out_ref = refs[:2], refs[2]
    for i in range(DT):
        place = slice(i * TILE, (i + 1) * TILE)
        k, at = (0, i) if i < CUT else (1, i - CUT)
        value = kept_ref[place, :] + received[k][at * TILE : (at + 1) * TILE, :].astype(jnp.float32)
        value = value + partner_ref[place, :].astype(jnp.float32)
        value = value + returned_ref[place, :].astype(jnp.float32)
        out_ref[place, :] = value.astype(jnp.bfloat16)


def finish(kept, partner_turned, returned, received):
    vmem = pl.BlockSpec(memory_space=pltpu.VMEM)
    return pl.pallas_call(
        finish_kernel,
        out_shape=jax.ShapeDtypeStruct((DV, DV), jnp.bfloat16),
        in_specs=[vmem] * 5,
        out_specs=vmem,
        compiler_params=pltpu.CompilerParams(vmem_limit_bytes=20 * MIB),
        cost_estimate=pl.CostEstimate(flops=DV * DV, bytes_accessed=DV * DV, transcendentals=0),
    )(*map(in_vmem, (kept, partner_turned, returned, *received)))


def local(amplitudes, exchange_ints, chol, domain, virt_energy, pair_energy):
    z = lax.axis_index("z")
    core = lax.axis_index("core")
    home = core == z // 2
    amps, exch = amplitudes[0], exchange_ints[0]
    column_group = ("z", "core")

    own = domain[0]
    flip_z = lambda pair: [(z * NC + c, (z ^ 1) * NC + (c ^ pair)) for z in range(NZ) for c in range(NC)]
    beside = lax.ppermute(own, column_group, flip_z(0))
    across = lax.ppermute(own, column_group, flip_z(1))
    swapped = core_swap(own)
    even, first_core = z % 2 == 0, core == 0
    mine = jnp.stack([jnp.where(even, own, beside), jnp.where(even, beside, own)])
    others = jnp.stack([jnp.where(even, swapped, across), jnp.where(even, across, swapped)])
    column = jnp.stack([jnp.where(first_core, mine, others), jnp.where(first_core, others, mine)])
    table = column.reshape(1, NZ * DT).astype(jnp.bfloat16)
    table = jnp.pad(table, ((0, SLICE - 1), (0, TILE - NZ * DT)))

    outgoing = with_table(spread(chol.reshape(2 * OWNERS, SLICE, NVT * TILE)), table)
    rows = lax.all_to_all(outgoing, ("x", "y"), 0, 0, tiled=True)
    rows = rows.reshape(NVT, SLICE, (NVT + 1) * TILE)

    early, _ = lax.optimization_barrier((amps, outgoing))
    moved = lax.ppermute(early, column_group, partner_perm(True))
    home_amps = lax.ppermute(early, column_group, home_perm(True))

    energies = jnp.take(virt_energy.reshape(NVT, TILE), own, axis=0).reshape(DV)
    base, turned = cycle_and_base(
        amps, exch, energies[None, :], (energies - pair_energy[0])[:, None], outgoing
    )

    moved, _ = lax.optimization_barrier((moved, turned))
    remote_amps = lax.ppermute(moved, column_group, home_perm(False))
    is_home = home.astype(jnp.int32)[None]
    home_amps, remote_amps = choose(is_home, (amps, remote_amps), (home_amps, moved))

    packed = pack(rows, home_amps, remote_amps, turned)
    arrived = lax.all_to_all(packed, ("z", "x", "y"), 0, 0, tiled=True)
    arrived = arrived.reshape(NZ, OWNERS, DT, SLICE, DV)

    turned_late, _ = lax.optimization_barrier((turned, arrived))
    partner_turned = lax.ppermute(turned_late, column_group, partner_perm(False))

    kept, sent, blocks = remote_ladder(remote_amps, arrived, turned)
    received = lax.ppermute(sent, column_group, home_perm(True))
    home_amps, partner_turned = lax.optimization_barrier((home_amps, partner_turned))
    begun = begin_ladder(home_amps, blocks)
    kept, begun = lax.optimization_barrier((kept, begun))
    finished = (kept + received.astype(jnp.float32)).astype(jnp.bfloat16)
    returned = lax.ppermute(finished, column_group, partner_perm(True))

    kept, *sent = home_ladder(is_home, home_amps, blocks, begun, base, finished)
    received = [lax.ppermute(part, column_group, home_perm(False)) for part in sent]
    return finish(kept, partner_turned, returned, received)[None]


def solution(mesh):
    finer = Mesh(mesh.devices.reshape(NZ, NC, NX, NY), ("z", "core", "x", "y"))
    group, everywhere = ("z", "core"), ("z", "core", "x", "y")
    placed = (
        P(everywhere, None, None),
        P(everywhere, None, None),
        P(group, ("x", "y"), None),
        P(everywhere, None),
        P(),
        P(everywhere),
    )
    return jax.shard_map(
        local, mesh=finer, in_specs=placed, out_specs=P(everywhere, None, None), check_vma=False
    )
```

```python
import functools

import jax
import jax.numpy as jnp
from jax import lax
from jax.experimental import pallas as pl
from jax.experimental.pallas import tpu as pltpu
from jax.sharding import Mesh
from jax.sharding import PartitionSpec as P

TILE = 128
NVT = 32
DT = 7
DV = DT * TILE
NZ, NC, NX, NY = 4, 2, 4, 4
OWNERS = NX * NY
SLICE = TILE // OWNERS
CHIPS = NZ * OWNERS
AFTER = 3
CUT = 4
BEGIN = 1
GROUP = 4
MIB = 1024 * 1024


def partner_perm(to_other_core):
    pairs = []
    for z in range(NZ):
        core = 1 - z // 2
        target = 1 - core if to_other_core else core
        pairs.append((z * NC + core, (z ^ 2) * NC + target))
    return pairs


def home_perm(from_home):
    pairs = [(z * NC + z // 2, z * NC + 1 - z // 2) for z in range(NZ)]
    return pairs if from_home else [(b, a) for a, b in pairs]


def core_swap(value):
    return lax.ppermute(value, "core", [(0, 1), (1, 0)])


def in_hbm(value):
    return pltpu.with_memory_space_constraint(value, pltpu.HBM)


def spread_kernel(chol_ref, out_ref, staged, in_sems, out_sems):
    arriving, leaving = [], []
    for m in range(OWNERS):
        for t in range(2):
            place = (m, t, slice(None), slice(0, NVT * TILE))
            arriving.append(
                pltpu.make_async_copy(
                    chol_ref.at[t * OWNERS + m], staged.at[m, t], in_sems.at[m, t]
                )
            )
            leaving.append(
                pltpu.make_async_copy(staged.at[m, t], out_ref.at[place], out_sems.at[m, t])
            )
    for copy in arriving:
        copy.start()
    for come, leave in zip(arriving, leaving):
        come.wait()
        leave.start()
    for copy in leaving:
        copy.wait()


def spread(chol):
    return pl.pallas_call(
        spread_kernel,
        out_shape=pltpu.HBM((OWNERS, 2, SLICE, (NVT + 1) * TILE), jnp.bfloat16),
        in_specs=[pl.BlockSpec(memory_space=pl.ANY)],
        out_specs=pl.BlockSpec(memory_space=pl.ANY),
        scratch_shapes=[
            pltpu.VMEM((OWNERS, 2, SLICE, NVT * TILE), jnp.bfloat16),
            pltpu.SemaphoreType.DMA((OWNERS, 2)),
            pltpu.SemaphoreType.DMA((OWNERS, 2)),
        ],
        compiler_params=pltpu.CompilerParams(vmem_limit_bytes=30 * MIB),
        cost_estimate=pl.CostEstimate(flops=0, bytes_accessed=4 * MIB, transcendentals=0),
    )(in_hbm(chol))


def table_kernel(table_ref, given_ref, out_ref, sems):
    del given_ref
    copies = []
    for m in range(OWNERS):
        for t in range(2):
            copies.append(
                pltpu.make_async_copy(
                    table_ref, out_ref.at[m, t, :, pl.ds(NVT * TILE, TILE)], sems.at[m, t]
                )
            )
    for copy in copies:
        copy.start()
    for copy in copies:
        copy.wait()


def with_table(spread_rows, table):
    anywhere = pl.BlockSpec(memory_space=pl.ANY)
    return pl.pallas_call(
        table_kernel,
        out_shape=pltpu.HBM(spread_rows.shape, jnp.bfloat16),
        in_specs=[pl.BlockSpec(memory_space=pltpu.VMEM), anywhere],
        out_specs=anywhere,
        scratch_shapes=[pltpu.SemaphoreType.DMA((OWNERS, 2))],
        input_output_aliases={1: 0},
        compiler_params=pltpu.CompilerParams(vmem_limit_bytes=8 * MIB),
    )(table, in_hbm(spread_rows))


def pack_kernel(given_ref, *refs):
    out_ref, rows_ref, given_tables, tables, tiles_ref, packed, row_sems, table_sems, sems = refs[AFTER:]
    beside = pltpu.make_async_copy(
        given_ref.at[:, :, pl.ds(NVT * TILE, TILE)], given_tables, table_sems.at[0]
    )
    beside.start()
    fetches = []
    for k in range(NVT // 4):
        part = pl.ds(k * 4, 4)
        fetches.append(
            pltpu.make_async_copy(
                given_ref.at[part, :, pl.ds(0, NVT * TILE)], rows_ref.at[part], row_sems.at[k]
            )
        )
    for fetch in fetches:
        fetch.start()
    beside.wait()
    for s in range(OWNERS):
        table = given_tables[2 * s].astype(jnp.float32).astype(jnp.int32)
        tables[s : s + 1, :] = table[0:1, :]
    move = pltpu.make_async_copy(tables, tiles_ref, table_sems.at[1])
    move.start()
    move.wait()
    for fetch in fetches:
        fetch.wait()

    def leave(group):
        dests = pl.ds(group * GROUP, GROUP)
        return pltpu.make_async_copy(packed.at[dests], out_ref.at[dests], sems.at[group])

    def one(group, carry):
        for k in range(GROUP):
            dest = group * GROUP + k
            z, s = dest // OWNERS, dest % OWNERS
            tiles = [tiles_ref[s, z * DT + t] for t in range(DT)]
            columns = [pl.multiple_of(tile * TILE, TILE) for tile in tiles]
            for i in range(DT):
                for j in range(DT):
                    packed[dest, i, :, j * TILE : (j + 1) * TILE] = rows_ref[
                        tiles[i], :, pl.ds(columns[j], TILE)
                    ]
        leave(group).start()
        return carry

    def gone(group, carry):
        leave(group).wait()
        return carry

    lax.fori_loop(0, CHIPS // GROUP, one, 0)
    lax.fori_loop(0, CHIPS // GROUP, gone, 0)


def pack(rows, *after):
    assert len(after) == AFTER
    shape = (CHIPS, DT, SLICE, DV)
    anywhere = pl.BlockSpec(memory_space=pl.ANY)
    return pl.pallas_call(
        pack_kernel,
        out_shape=pltpu.HBM(shape, jnp.bfloat16),
        in_specs=[anywhere] * (1 + AFTER),
        out_specs=anywhere,
        scratch_shapes=[
            pltpu.VMEM((NVT, SLICE, NVT * TILE), jnp.bfloat16),
            pltpu.VMEM((NVT, SLICE, TILE), jnp.bfloat16),
            pltpu.VMEM((OWNERS, TILE), jnp.int32),
            pltpu.SMEM((OWNERS, TILE), jnp.int32),
            pltpu.VMEM(shape, jnp.bfloat16),
            pltpu.SemaphoreType.DMA((NVT // 4,)),
            pltpu.SemaphoreType.DMA((2,)),
            pltpu.SemaphoreType.DMA((CHIPS // GROUP,)),
        ],
        compiler_params=pltpu.CompilerParams(vmem_limit_bytes=30 * MIB),
        cost_estimate=pl.CostEstimate(
            flops=0, bytes_accessed=4 * CHIPS * DT * SLICE * DV, transcendentals=0
        ),
    )(*map(in_hbm, (rows, *after)))


def cycle_kernel(
    domain_ref, pair_ref, amps_ref, exch_all_ref, exch_ref, energy_ref, after_ref, base_ref, turned_ref
):
    del after_ref
    cycle = jnp.dot(amps_ref[...], exch_all_ref[...], preferred_element_type=jnp.float32)
    cycle = cycle.astype(jnp.bfloat16).astype(jnp.float32)
    energies = [energy_ref[pl.ds(domain_ref[t], 1), :] for t in range(DT)]
    here = energy_ref[pl.ds(domain_ref[pl.program_id(0)], 1), :]
    column = jnp.broadcast_to(here, (TILE, TILE)).T[:, 0:1] - pair_ref[0]
    denominator = column + jnp.concatenate(energies, axis=1)
    base_ref[...] = (
        exch_ref[...].astype(jnp.float32)
        + denominator * amps_ref[...].astype(jnp.float32)
        + cycle
    )
    turned_ref[...] = cycle.T.astype(jnp.bfloat16)


def cycle_and_base(domain, pair_energy, amps, exch, energies, after):
    return pl.pallas_call(
        cycle_kernel,
        out_shape=(pltpu.HBM((DV, DV), jnp.float32), pltpu.HBM((DV, DV), jnp.bfloat16)),
        grid=(DT,),
        in_specs=[
            pl.BlockSpec(memory_space=pltpu.SMEM),
            pl.BlockSpec(memory_space=pltpu.SMEM),
            pl.BlockSpec((TILE, DV), lambda i: (i, 0)),
            pl.BlockSpec((DV, DV), lambda i: (0, 0)),
            pl.BlockSpec((TILE, DV), lambda i: (i, 0)),
            pl.BlockSpec((NVT, TILE), lambda i: (0, 0)),
            pl.BlockSpec(memory_space=pl.ANY),
        ],
        out_specs=(
            pl.BlockSpec((TILE, DV), lambda i: (i, 0)),
            pl.BlockSpec((DV, TILE), lambda i: (0, i)),
        ),
        compiler_params=pltpu.CompilerParams(vmem_limit_bytes=32 * MIB),
        cost_estimate=pl.CostEstimate(
            flops=2 * DV**3, bytes_accessed=14 * DV * DV, transcendentals=0
        ),
    )(domain, pair_energy, amps, exch, exch, energies, in_hbm(after))


def choose_kernel(home_ref, *refs):
    sources, targets, sems = (refs[:2], refs[2:4]), refs[4:6], refs[6]
    home = home_ref[0] > 0

    def copies(which):
        made = []
        for k in range(2):
            for i in range(DT):
                place = pl.ds(i * TILE, TILE)
                made.append(
                    pltpu.make_async_copy(
                        sources[which][k].at[place], targets[k].at[place], sems.at[k, i]
                    )
                )
        return made

    for which in range(2):

        @pl.when(home if which == 0 else jnp.logical_not(home))
        def _(which=which):
            made = copies(which)
            for copy in made:
                copy.start()
            for copy in made:
                copy.wait()


def choose(home, at_home, elsewhere):
    vmem = pl.BlockSpec(memory_space=pltpu.VMEM)
    return pl.pallas_call(
        choose_kernel,
        out_shape=[pltpu.VMEM((DV, DV), jnp.bfloat16)] * 2,
        in_specs=[pl.BlockSpec(memory_space=pltpu.SMEM)] + [pl.BlockSpec(memory_space=pl.ANY)] * 4,
        out_specs=[vmem, vmem],
        scratch_shapes=[pltpu.SemaphoreType.DMA((2, DT))],
        compiler_params=pltpu.CompilerParams(vmem_limit_bytes=8 * MIB),
        cost_estimate=pl.CostEstimate(flops=0, bytes_accessed=4 * DV * DV, transcendentals=0),
    )(home, *at_home, *elsewhere)


def ladder_products(vectors, amps_ref, block_ref, half, total, so_far, ready, give):
    ready(vectors[0])
    for q in vectors:
        half[...] = lax.dot_general(
            amps_ref[...],
            block_ref[q],
            (((1,), (1,)), ((), ())),
            preferred_element_type=jnp.float32,
        ).astype(jnp.bfloat16)
        if q < vectors[-1]:
            ready(q + 1)
        for i, (start, stop) in enumerate(((0, CUT), (CUT, DT))):
            place = slice(start * TILE, stop * TILE)
            part = jnp.dot(
                block_ref[q, place, :], half[...], preferred_element_type=jnp.float32
            )
            if q > vectors[0]:
                part = part + total[place, :]
            elif so_far is not None:
                part = part + so_far[place, :]
            if q < vectors[-1]:
                total[place, :] = part
            else:
                give(i, place, part)


def put(part, i, first_ref, second_ref):
    target = first_ref if i == 0 else second_ref
    target[...] = part.astype(jnp.bfloat16)


def remote_kernel(amps_ref, given_ref, added_ref, *refs):
    kept_ref, sent_ref, block_ref, half, total, landed, sems = refs
    copies = [
        [
            pltpu.make_async_copy(given_ref.at[q, :, i], landed.at[q, i], sems.at[q, i])
            for i in range(DT)
        ]
        for q in range(NZ)
    ]
    for q in range(NZ):
        for copy in copies[q]:
            copy.start()

    def ready(q):
        for copy in copies[q]:
            copy.wait()
        for i in range(DT):
            tile = landed[q, i].astype(jnp.float32).reshape(TILE, DV)
            block_ref[q, i * TILE : (i + 1) * TILE, :] = tile.astype(jnp.bfloat16)

    def give(i, place, part):
        kept_ref[place, :] = part
        sent_ref[place, :] = (part + added_ref[place, :].astype(jnp.float32)).astype(jnp.bfloat16)

    ladder_products(range(NZ), amps_ref, block_ref, half, total, None, ready, give)


def begin_kernel(amps_ref, block_ref, total_ref, half):
    def give(i, place, part):
        total_ref[place, :] = part

    ladder_products(range(BEGIN), amps_ref, block_ref, half, total_ref, None, lambda q: None, give)


def home_kernel(home_ref, amps_ref, block_ref, so_far_ref, added_ref, after_ref, *refs):
    del after_ref
    kept_ref, first_ref, second_ref, half, total = refs
    keep = (home_ref[0] > 0).astype(jnp.float32)

    def give(i, place, part):
        kept_ref[place, :] = added_ref[place, :] + keep * part
        put(part, i, first_ref, second_ref)

    ladder_products(
        range(BEGIN, NZ), amps_ref, block_ref, half, total, so_far_ref, lambda q: None, give
    )


def in_vmem(value):
    return pltpu.with_memory_space_constraint(value, pltpu.VMEM)


def ladder_cost(vectors):
    return pl.CostEstimate(
        flops=4 * vectors * DV**3, bytes_accessed=2 * vectors * DV * DV, transcendentals=0
    )


def remote_ladder(amps, arrived, turned):
    vmem, anywhere = pl.BlockSpec(memory_space=pltpu.VMEM), pl.BlockSpec(memory_space=pl.ANY)
    out_shape = [
        pltpu.VMEM((DV, DV), jnp.float32),
        pltpu.VMEM((DV, DV), jnp.bfloat16),
        pltpu.VMEM((NZ, DV, DV), jnp.bfloat16),
    ]
    return pl.pallas_call(
        remote_kernel,
        out_shape=out_shape,
        in_specs=[vmem, anywhere, vmem],
        out_specs=[vmem] * len(out_shape),
        scratch_shapes=[
            pltpu.VMEM((DV, DV), jnp.bfloat16),
            pltpu.VMEM((DV, DV), jnp.float32),
            pltpu.VMEM((NZ, DT, OWNERS, SLICE, DV), jnp.bfloat16),
            pltpu.SemaphoreType.DMA((NZ, DT)),
        ],
        compiler_params=pltpu.CompilerParams(vmem_limit_bytes=20 * MIB),
        cost_estimate=ladder_cost(NZ),
    )(in_vmem(amps), in_hbm(arrived), in_vmem(turned))


def begin_ladder(amps, blocks):
    vmem = pl.BlockSpec(memory_space=pltpu.VMEM)
    return pl.pallas_call(
        begin_kernel,
        out_shape=pltpu.VMEM((DV, DV), jnp.float32),
        in_specs=[vmem] * 2,
        out_specs=vmem,
        scratch_shapes=[pltpu.VMEM((DV, DV), jnp.bfloat16)],
        compiler_params=pltpu.CompilerParams(vmem_limit_bytes=20 * MIB),
        cost_estimate=ladder_cost(BEGIN),
    )(in_vmem(amps), in_vmem(blocks))


def home_ladder(home, amps, blocks, so_far, base, after):
    vmem, anywhere = pl.BlockSpec(memory_space=pltpu.VMEM), pl.BlockSpec(memory_space=pl.ANY)
    out_shape = [
        pltpu.VMEM((DV, DV), jnp.float32),
        pltpu.VMEM((CUT * TILE, DV), jnp.bfloat16),
        pltpu.VMEM((DV - CUT * TILE, DV), jnp.bfloat16),
    ]
    return pl.pallas_call(
        home_kernel,
        out_shape=out_shape,
        in_specs=[pl.BlockSpec(memory_space=pltpu.SMEM)] + [vmem] * 4 + [anywhere],
        out_specs=[vmem] * len(out_shape),
        scratch_shapes=[pltpu.VMEM((DV, DV), jnp.bfloat16), pltpu.VMEM((DV, DV), jnp.float32)],
        compiler_params=pltpu.CompilerParams(vmem_limit_bytes=20 * MIB),
        cost_estimate=ladder_cost(NZ - BEGIN),
    )(home, *map(in_vmem, (amps, blocks, so_far, base)), after)


def finish_kernel(kept_ref, partner_ref, returned_ref, *refs):
    received, out_ref = refs[:2], refs[2]
    for i in range(DT):
        place = slice(i * TILE, (i + 1) * TILE)
        k, at = (0, i) if i < CUT else (1, i - CUT)
        value = kept_ref[place, :] + received[k][at * TILE : (at + 1) * TILE, :].astype(jnp.float32)
        value = value + partner_ref[place, :].astype(jnp.float32)
        value = value + returned_ref[place, :].astype(jnp.float32)
        out_ref[place, :] = value.astype(jnp.bfloat16)


def finish(kept, partner_turned, returned, received):
    vmem = pl.BlockSpec(memory_space=pltpu.VMEM)
    return pl.pallas_call(
        finish_kernel,
        out_shape=jax.ShapeDtypeStruct((DV, DV), jnp.bfloat16),
        in_specs=[vmem] * 5,
        out_specs=vmem,
        compiler_params=pltpu.CompilerParams(vmem_limit_bytes=20 * MIB),
        cost_estimate=pl.CostEstimate(flops=DV * DV, bytes_accessed=DV * DV, transcendentals=0),
    )(*map(in_vmem, (kept, partner_turned, returned, *received)))


def local(amplitudes, exchange_ints, chol, domain, virt_energy, pair_energy):
    z = lax.axis_index("z")
    core = lax.axis_index("core")
    home = core == z // 2
    amps, exch = amplitudes[0], exchange_ints[0]
    column_group = ("z", "core")

    own = domain[0]
    flip_z = lambda pair: [(z * NC + c, (z ^ 1) * NC + (c ^ pair)) for z in range(NZ) for c in range(NC)]
    beside = lax.ppermute(own, column_group, flip_z(0))
    across = lax.ppermute(own, column_group, flip_z(1))
    swapped = core_swap(own)
    even, first_core = z % 2 == 0, core == 0
    mine = jnp.stack([jnp.where(even, own, beside), jnp.where(even, beside, own)])
    others = jnp.stack([jnp.where(even, swapped, across), jnp.where(even, across, swapped)])
    column = jnp.stack([jnp.where(first_core, mine, others), jnp.where(first_core, others, mine)])
    table = column.reshape(1, NZ * DT).astype(jnp.bfloat16)
    table = jnp.pad(table, ((0, SLICE - 1), (0, TILE - NZ * DT)))

    outgoing = with_table(spread(chol.reshape(2 * OWNERS, SLICE, NVT * TILE)), table)
    rows = lax.all_to_all(outgoing, ("x", "y"), 0, 0, tiled=True)
    rows = rows.reshape(NVT, SLICE, (NVT + 1) * TILE)

    early, _ = lax.optimization_barrier((amps, outgoing))
    moved = lax.ppermute(early, column_group, partner_perm(True))
    home_amps = lax.ppermute(early, column_group, home_perm(True))

    base, turned = cycle_and_base(
        own, pair_energy, amps, exch, virt_energy.reshape(NVT, TILE), outgoing
    )

    moved, _ = lax.optimization_barrier((moved, turned))
    remote_amps = lax.ppermute(moved, column_group, home_perm(False))
    is_home = home.astype(jnp.int32)[None]
    home_amps, remote_amps = choose(is_home, (amps, remote_amps), (home_amps, moved))

    packed = pack(rows, home_amps, remote_amps, turned)
    arrived = lax.all_to_all(packed, ("z", "x", "y"), 0, 0, tiled=True)
    arrived = arrived.reshape(NZ, OWNERS, DT, SLICE, DV)

    turned_late, _ = lax.optimization_barrier((turned, arrived))
    partner_turned = lax.ppermute(turned_late, column_group, partner_perm(False))

    kept, sent, blocks = remote_ladder(remote_amps, arrived, turned)
    received = lax.ppermute(sent, column_group, home_perm(True))
    home_amps, partner_turned = lax.optimization_barrier((home_amps, partner_turned))
    begun = begin_ladder(home_amps, blocks)
    kept, begun = lax.optimization_barrier((kept, begun))
    finished = (kept + received.astype(jnp.float32)).astype(jnp.bfloat16)
    returned = lax.ppermute(finished, column_group, partner_perm(True))

    kept, *sent = home_ladder(is_home, home_amps, blocks, begun, base, finished)
    received = [lax.ppermute(part, column_group, home_perm(False)) for part in sent]
    return finish(kept, partner_turned, returned, received)[None]


def solution(mesh):
    finer = Mesh(mesh.devices.reshape(NZ, NC, NX, NY), ("z", "core", "x", "y"))
    group, everywhere = ("z", "core"), ("z", "core", "x", "y")
    placed = (
        P(everywhere, None, None),
        P(everywhere, None, None),
        P(group, ("x", "y"), None),
        P(everywhere, None),
        P(),
        P(everywhere),
    )
    return jax.shard_map(
        local, mesh=finer, in_specs=placed, out_specs=P(everywhere, None, None), check_vma=False
    )
```
